256 devices in a mesh: sub: 32 (over y, x, core), grp: 8 (over z).
Axes of the slice: x: 4, y: 4, z: 8, core: 2. Of those that a mesh axis runs over, the one named last changes fastest.
Arguments:
- residual: bfloat16 [8, 32, 1024, 512], P('grp', 'sub'), may hold values from -6 to 6
- face_order: int32 [8, 32, 1024], P('grp', 'sub'), may hold values from 0 to 1023, each once within a row
- stiffness: float32 [8, 32], replicated, may hold values from 1 to 100
- schur: bfloat16 [8, 32, 1024, 1024], P('grp', 'sub')
- local_inverse: bfloat16 [8, 32, 1024, 1024], P('grp', 'sub')
- coarse_basis: bfloat16 [8, 32, 1024, 128], P('grp', 'sub'), may hold values from -0.1875 to 0.1875
- coarse_map: int32 [8, 32, 128], P('grp', 'sub'), may hold values from 0 to 511, as said below
- level2_inverse: float32 [8, 512, 512], P('grp')
- level2_basis: float32 [8, 512, 128], P('grp'), may hold values from -0.25 to 0.25
- level2_map: int32 [8, 128], P('grp'), may hold values from 0 to 511, as said below
- level3_inverse: float32 [512, 512], replicated
Outputs:
- solution: bfloat16 [8, 32, 1024, 512], P('grp', 'sub')
- image: bfloat16 [8, 32, 1024, 512], P('grp', 'sub')
The draws below stay inside these ranges and needn't reach their ends.
Inputs may be any that keep to these rules, and one draw needn't show every extreme that they name: `face_order`: each subdomain's row holds every number of 0 to 1023 once. `coarse_map`: within one subdomain the 128 entries are distinct, and each of a group's 512 level-2 coarse values is named by some subdomain of the group. `level2_map`: within one group the 128 entries are distinct, and each level-3 coarse value is named by some group.
All inputs are finite; a program needn't handle non-finite values.
Results may differ from the reference program's by a relative error of at most 0.0062.
Values may be sent and summed in bfloat16 or wider, within the bound.
A program may use at most 64 MiB of HBM per device.

```python
import math
import jax
import jax.numpy as jnp
from jax import lax

IF = 1024
K = 512
NC1 = 128
NC2 = 128
GROUPS = 8
SUBS = 32
NG2 = 512
NG3 = 512


def symmetric_block(noise_draw, diagonal, spread):
    extent = noise_draw.shape[-1]
    identity = jnp.eye(extent, dtype=jnp.float32)
    off_part = (noise_draw + jnp.swapaxes(noise_draw, -1, -2)) * (spread / math.sqrt(2.0 * extent))
    return off_part * (1.0 - identity) + diagonal[..., None] * identity


def log_spread(key_range, full_shape, low, high):
    return jnp.exp(jax.random.uniform(key_range, full_shape, jnp.float32, math.log(low), math.log(high)))


def draw_schur(key, part):
    key = jax.random.fold_in(key, 31)
    key_noise, key_diag = jax.random.split(key)
    full_shape = (GROUPS, SUBS, IF, IF)
    noise_draw = jax.random.normal(key_noise, full_shape, jnp.float32)
    return symmetric_block(noise_draw, log_spread(key_diag, full_shape[:-1], 1.0, 4.0), 0.8).astype(jnp.bfloat16)


def draw_local_inverse(key, part):
    key = jax.random.fold_in(key, 37)
    key_noise, key_diag = jax.random.split(key)
    full_shape = (GROUPS, SUBS, IF, IF)
    noise_draw = jax.random.normal(key_noise, full_shape, jnp.float32)
    return symmetric_block(noise_draw, log_spread(key_diag, full_shape[:-1], 0.3, 1.0), 0.4).astype(jnp.bfloat16)


def draw_level2_inverse(key, part):
    key = jax.random.fold_in(key, 41)
    key_noise, key_diag = jax.random.split(key)
    full_shape = (GROUPS, NG2, NG2)
    noise_draw = jax.random.normal(key_noise, full_shape, jnp.float32)
    return symmetric_block(noise_draw, log_spread(key_diag, full_shape[:-1], 0.1, 0.4), 0.1)


def draw_level3_inverse(key, part):
    key = jax.random.fold_in(key, 43)
    key_noise, key_diag = jax.random.split(key)
    full_shape = (NG3, NG3)
    noise_draw = jax.random.normal(key_noise, full_shape, jnp.float32)
    return symmetric_block(noise_draw, log_spread(key_diag, full_shape[:-1], 0.1, 0.4), 0.1)


def group_shuffle(group_key):
    return jax.random.permutation(group_key, NG2)


def draw_coarse_map(key, part):
    key = jax.random.fold_in(key, 53)
    group_keys = jax.random.split(key, GROUPS)
    shuffled = jax.vmap(group_shuffle)(group_keys)
    windows = (jnp.arange(SUBS)[:, None] * (NC1 // 8) + jnp.arange(NC1)[None, :]) % NG2
    return shuffled[:, windows].astype(jnp.int32)


def draw_level2_map(key, part):
    key = jax.random.fold_in(key, 59)
    shuffled = jax.random.permutation(key, NG3)
    windows = (jnp.arange(GROUPS)[:, None] * (NC2 // 2) + jnp.arange(NC2)[None, :]) % NG3
    return shuffled[windows].astype(jnp.int32)


def block_scale(own_key, dims, cuts, low, high):
    level = 1.0
    for dim, shards_of in cuts:
        steps = jax.random.uniform(jax.random.fold_in(jax.random.fold_in(own_key, 6), dim), (shards_of,), jnp.float32, low / len(cuts), high / len(cuts))
        level = level * jnp.repeat(jnp.exp(steps), dims[dim] // shards_of).reshape((-1,) + (1,) * (len(dims) - 1 - dim))
    return level


def scatter_about(stream_key, shape, deviation, reach, shards=(), kind=jnp.bfloat16):
    loudness = block_scale(stream_key, shape, shards, -0.22, 0.18) if shards else 1.0
    values = jax.random.normal(stream_key, shape, jnp.float32) * deviation * loudness
    return jnp.minimum(jnp.maximum(values, -reach), reach).astype(kind)


def setup_inputs(seed: int = 0) -> dict:
    seeds = jax.random.split(jax.random.key(seed), 12)
    return {
        "residual": scatter_about(seeds[0], (GROUPS, SUBS, IF, K), 1.0, 6.0, ((0, 8), (1, 32))),
        "face_order": jax.vmap(lambda own: jax.random.permutation(own, IF))(jax.random.split(seeds[1], GROUPS * SUBS)).reshape((GROUPS, SUBS, IF)).astype(jnp.int32),
        "stiffness": jnp.clip(jnp.exp(jax.random.uniform(seeds[2], (GROUPS, SUBS), jnp.float32, math.log(1.0), math.log(100.0))), 1.0, 100.0),
        "schur": draw_schur(jax.random.fold_in(seeds[11], 71), 0),
        "local_inverse": draw_local_inverse(jax.random.fold_in(seeds[11], 71), 0),
        "coarse_basis": scatter_about(seeds[5], (GROUPS, SUBS, IF, NC1), IF ** -0.5, 0.1875, ((0, 8), (1, 32))),
        "coarse_map": draw_coarse_map(jax.random.fold_in(seeds[11], 71), 0),
        "level2_inverse": draw_level2_inverse(jax.random.fold_in(seeds[11], 71), 0),
        "level2_basis": scatter_about(seeds[8], (GROUPS, NG2, NC2), NG2 ** -0.5, 0.25, ((0, 8),), jnp.float32),
        "level2_map": draw_level2_map(jax.random.fold_in(seeds[11], 71), 0),
        "level3_inverse": draw_level3_inverse(jax.random.fold_in(seeds[11], 71), 0),
    }


highest = lax.Precision.HIGHEST


def face_weights(stiffness):
    zero_column = jnp.zeros_like(stiffness[:, :1])
    zero_row = jnp.zeros_like(stiffness[:1, :])
    lower_member = jnp.concatenate([zero_column, stiffness[:, :-1]], axis=1)
    upper_member = jnp.concatenate([stiffness[:, 1:], zero_column], axis=1)
    lower_group = jnp.concatenate([zero_row, stiffness[:-1, :]], axis=0)
    upper_group = jnp.concatenate([stiffness[1:, :], zero_row], axis=0)
    neighbours = jnp.stack([lower_member, upper_member, lower_group, upper_group], axis=-1)
    group_count, member_count = stiffness.shape
    member_pos = jnp.broadcast_to(jnp.arange(member_count)[None, :], stiffness.shape)
    group_pos = jnp.broadcast_to(jnp.arange(group_count)[:, None], stiffness.shape)
    present = jnp.stack([member_pos > 0, member_pos < member_count - 1, group_pos > 0, group_pos < group_count - 1], axis=-1)
    return jnp.where(present, stiffness[..., None] / (stiffness[..., None] + neighbours), jnp.float32(1.0))


def dof_weights(ordering, weights):
    inverse = jnp.argsort(ordering, axis=-1).astype(jnp.int32)
    faces = (inverse // (IF // 4)).astype(jnp.int32)
    return inverse, jnp.take_along_axis(weights, faces, axis=-1)


def weighted_residual(residual_g, ordering_g, weights_g):
    inverse, dof_weight = dof_weights(ordering_g, weights_g)
    weighted = (dof_weight[..., None] * residual_g.astype(jnp.float32)).astype(jnp.bfloat16)
    return dof_weight, weighted


def level2_term(inputs):
    residual_g, ordering_g, weights_g, basis_g, map_g = inputs
    dof_weight, weighted = weighted_residual(residual_g, ordering_g, weights_g)
    coarse_res = jnp.einsum("sic,sik->sck", basis_g.astype(jnp.float32), weighted.astype(jnp.float32), precision=highest)
    total = jnp.zeros((NG2, K), jnp.float32)
    return total.at[map_g.reshape(-1)].add(coarse_res.reshape(-1, K))


def sent_faces(inputs):
    residual_g, ordering_g, weights_g, inverse_g, basis_g, map_g, solution_g = inputs
    dof_weight, weighted = weighted_residual(residual_g, ordering_g, weights_g)
    local_part = jnp.einsum("sij,sjk->sik", inverse_g.astype(jnp.float32), weighted.astype(jnp.float32), precision=highest)
    coarse_part = jnp.einsum("sic,sck->sik", basis_g.astype(jnp.float32), solution_g[map_g], precision=highest)
    sendable = (dof_weight[..., None] * (local_part + coarse_part)).astype(jnp.bfloat16)
    permuted = jnp.take_along_axis(sendable, ordering_g[..., None], axis=1)
    return permuted.reshape(SUBS, 4, IF // 4, K)


def assemble(inputs):
    blocks_g, lower_g, upper_g, ordering_g, schur_g = inputs
    zero_member = jnp.zeros_like(blocks_g[:1, 0])
    from_lower = jnp.concatenate([zero_member, blocks_g[:-1, 1]], axis=0)
    from_upper = jnp.concatenate([blocks_g[1:, 0], zero_member], axis=0)
    received = jnp.stack([from_lower, from_upper, lower_g, upper_g], axis=1)
    summed = (blocks_g.astype(jnp.float32) + received.astype(jnp.float32)).astype(jnp.bfloat16).reshape(SUBS, IF, K)
    inverse = jnp.argsort(ordering_g, axis=-1).astype(jnp.int32)
    solution = jnp.take_along_axis(summed, inverse[..., None], axis=1)
    image = jnp.einsum("sij,sjk->sik", schur_g.astype(jnp.float32), solution.astype(jnp.float32), precision=highest)
    return solution, image.astype(jnp.bfloat16)


def reference(residual, face_order, stiffness, schur, local_inverse, coarse_basis, coarse_map, level2_inverse, level2_basis, level2_map, level3_inverse):
    weights = jnp.broadcast_to(face_weights(stiffness)[:, :, None, :], (GROUPS, SUBS, 1, 4))[:, :, 0, :]
    level2_res = lax.map(level2_term, (residual, face_order, weights, coarse_basis, coarse_map))
    level3_terms = jnp.einsum("gnc,gnk->gck", level2_basis, level2_res, precision=highest)
    level3_res = jnp.zeros((NG3, K), jnp.float32).at[level2_map.reshape(-1)].add(level3_terms.reshape(-1, K))
    level3_sol = jnp.dot(level3_inverse, level3_res, precision=highest)
    level2_sol = jnp.einsum("gnm,gmk->gnk", level2_inverse, level2_res, precision=highest)
    level2_sol = level2_sol + jnp.einsum("gnc,gck->gnk", level2_basis, level3_sol[level2_map], precision=highest)
    blocks = lax.map(sent_faces, (residual, face_order, weights, local_inverse, coarse_basis, coarse_map, level2_sol))
    zero_group = jnp.zeros_like(blocks[:1, :, 0])
    from_lower_group = jnp.concatenate([zero_group, blocks[:-1, :, 3]], axis=0)
    from_upper_group = jnp.concatenate([blocks[1:, :, 2], zero_group], axis=0)
    solution, image = lax.map(assemble, (blocks, from_lower_group, from_upper_group, face_order, schur))
    return solution, image
```

```python
import functools

import jax
import jax.numpy as jnp
from jax import lax
from jax.experimental import pallas as pl
from jax.experimental.pallas import tpu as pltpu
from jax.sharding import PartitionSpec as P

MESH = pl.DeviceIdType.MESH
F32 = jnp.float32
BF16 = jnp.bfloat16
LANES = 128


def dot(a, b):
    return jnp.dot(a, b, preferred_element_type=F32)


def dot_t(a, b):
    return lax.dot_general(a, b, (((1,), (1,)), ((), ())), preferred_element_type=F32)


def two_terms(x):
    high = x.astype(BF16)
    low = (x - high.astype(F32)).astype(BF16)
    return jnp.concatenate([high, low], axis=0)


def fold_terms(x):
    half = x.shape[0] // 2
    return x[:half] + x[half:]


def block(index, size):
    return pl.ds(pl.multiple_of(index * size, size), size)


def kernel(
    nsub,
    ngrp,
    resid_h,
    order_h,
    stiff_h,
    schur_h,
    linv_h,
    basis_h,
    cmap_h,
    l2inv_h,
    l2basis_h,
    l2map_h,
    l3inv_h,
    sol_h,
    img_h,
    resid,
    order,
    stiff,
    schur,
    linv,
    basis,
    cmap,
    l2inv,
    l2basis,
    l2map,
    l3inv,
    cmaps,
    l2maps,
    wcol,
    perm_t,
    perm,
    weighted,
    cres_t,
    recv2,
    onehot2,
    b2,
    onehot3,
    q3,
    recv3,
    term3,
    pre,
    back,
    xcoef,
    basis_f,
    local_f,
    schur_p,
    mine,
    theirs,
    sol_acc,
    img_acc,
    sol,
    img,
    in_sem,
    out_sem,
    map2_sem,
    map3_sem,
    a2a_sem,
    z_sem,
    back_sem,
    face_send,
    face_recv,
):
    grp = lax.axis_index("grp")
    sub = lax.axis_index("sub")
    n_if, cols = resid.shape
    face = n_if // 4
    nc1 = basis.shape[1]
    nc2 = l2basis.shape[1]
    ng2 = l2basis.shape[0]
    ng3 = l3inv.shape[0]
    kc = cols // nsub
    half = cols // 2

    loads = [
        pltpu.make_async_copy(src, dst, in_sem.at[i])
        for i, (src, dst) in enumerate(
            [
                (order_h.at[0], order),
                (stiff_h, stiff),
                (cmap_h.at[0], cmap),
                (l2map_h, l2map),
                (resid_h.at[0, 0], resid),
                (basis_h.at[0, 0], basis),
                (l2basis_h.at[0], l2basis),
                (l3inv_h, l3inv),
                (linv_h.at[0, 0], linv),
                (l2inv_h.at[0], l2inv),
                (schur_h.at[0, 0], schur),
            ]
        )
    ]
    for load in loads:
        load.start()
    (ld_order, ld_stiff, ld_cmap, ld_l2map, ld_resid, ld_basis, ld_l2basis, ld_l3inv, ld_linv, ld_l2inv, ld_schur) = loads

    barrier = pltpu.get_barrier_semaphore()

    def greet_sub(j, carry):
        pl.semaphore_signal(barrier, inc=1, device_id={"sub": lax.rem(sub + j, nsub)}, device_id_type=MESH)
        return carry

    def greet_grp(j, carry):
        pl.semaphore_signal(barrier, inc=1, device_id={"grp": lax.rem(grp + j, ngrp)}, device_id_type=MESH)
        return carry

    lax.fori_loop(1, nsub, greet_sub, 0)
    lax.fori_loop(1, ngrp, greet_grp, 0)

    ld_stiff.wait()
    own = stiff[grp, sub]

    def weight(g, s, present):
        other = stiff[jnp.clip(g, 0, ngrp - 1), jnp.clip(s, 0, nsub - 1)]
        num = jnp.full((8, LANES), own, F32)
        den = num + jnp.full((8, LANES), other, F32)
        return jnp.where(jnp.full((8, LANES), present, jnp.int32) > 0, num / den, F32(1.0))

    exists = [sub > 0, sub < nsub - 1, grp > 0, grp < ngrp - 1]
    weights = [
        weight(grp, sub - 1, exists[0].astype(jnp.int32)),
        weight(grp, sub + 1, exists[1].astype(jnp.int32)),
        weight(grp - 1, sub, exists[2].astype(jnp.int32)),
        weight(grp + 1, sub, exists[3].astype(jnp.int32)),
    ]
    for f in range(4):
        high = weights[f].astype(BF16)
        low = (weights[f] - high.astype(F32)).astype(BF16)
        pair = jnp.concatenate([high[0:1], low[0:1]], axis=1)
        wcol[f * face : (f + 1) * face, :] = jnp.broadcast_to(pair, (face, 2 * LANES))

    ld_order.wait()
    ld_basis.wait()
    ld_resid.wait()

    def weigh(r, carry):
        rows = block(r, face)
        ids = lax.broadcasted_iota(jnp.int32, (face, n_if), 0) + r * face
        pt = jnp.where(ids == order[...], F32(1.0), F32(0.0)).astype(BF16)
        perm_t[rows, :] = pt
        both = dot(pt, wcol[...])
        dofw = both[:, :LANES] + both[:, LANES:]
        res = resid[rows, :].astype(F32)
        reps = -(-cols // LANES)
        wide = jnp.concatenate([dofw] * reps, axis=1)[:, :cols]
        weighted[rows, :] = (wide * res).astype(BF16)
        return carry

    lax.fori_loop(0, 4, weigh, 0)
    coarse = dot(basis[...].astype(F32).T.astype(BF16), weighted[...])
    cres_t[...] = coarse.T.astype(BF16)

    ld_cmap.wait()
    ld_l2map.wait()
    cmaps[sub] = jnp.broadcast_to(cmap[...], (8, nc1))
    l2maps[grp] = jnp.broadcast_to(l2map[...], (8, nc2))
    pl.semaphore_wait(barrier, nsub + ngrp - 2)

    def send_map2(j, carry):
        t = lax.rem(sub + j, nsub)
        pltpu.make_async_remote_copy(
            src_ref=cmaps.at[sub],
            dst_ref=cmaps.at[sub],
            send_sem=map2_sem.at[0],
            recv_sem=map2_sem.at[1],
            device_id={"sub": t},
            device_id_type=MESH,
        ).start()
        return carry

    def send_map3(j, carry):
        t = lax.rem(grp + j, ngrp)
        pltpu.make_async_remote_copy(
            src_ref=l2maps.at[grp],
            dst_ref=l2maps.at[grp],
            send_sem=map3_sem.at[0],
            recv_sem=map3_sem.at[1],
            device_id={"grp": t},
            device_id_type=MESH,
        ).start()
        return carry

    def send_a2a(j, carry):
        t = lax.rem(sub + j, nsub)
        pltpu.make_async_remote_copy(
            src_ref=cres_t.at[block(t, kc), :],
            dst_ref=recv2.at[:, block(sub, nc1)],
            send_sem=a2a_sem.at[0],
            recv_sem=a2a_sem.at[1],
            device_id={"sub": t},
            device_id_type=MESH,
        ).start()
        return carry

    lax.fori_loop(1, nsub, send_map2, 0)
    lax.fori_loop(1, nsub, send_a2a, 0)
    lax.fori_loop(1, ngrp, send_map3, 0)
    recv2[:, block(sub, nc1)] = cres_t[block(sub, kc), :]

    def wait_bytes(ref, sem):
        pltpu.make_async_copy(ref, ref, sem).wait()

    wait_bytes(cmaps.at[pl.ds(0, nsub - 1)], map2_sem.at[1])

    def build2(t, carry):
        ids = lax.broadcasted_iota(jnp.int32, (ng2, nc1), 0)
        onehot2[:, block(t, nc1)] = jnp.where(ids == cmaps[t][0:1], F32(1.0), F32(0.0)).astype(BF16)
        return carry

    lax.fori_loop(0, nsub, build2, 0)

    ld_l2basis.wait()
    l2basis_t = l2basis[...].T.astype(BF16)
    wide2 = min(1024, nsub * nc1)

    def gather2(j, carry):
        b2[:, block(j, wide2)] = dot(l2basis_t, onehot2[:, block(j, wide2)]).astype(BF16)
        return carry

    lax.fori_loop(0, nsub * nc1 // wide2, gather2, 0)

    wait_bytes(recv2.at[:, pl.ds(0, (nsub - 1) * nc1)], a2a_sem.at[1])
    term3[...] = dot_t(recv2[...], b2[...])
    recv3[:, block(grp, nc2)] = term3[...]

    def send_z(j, carry):
        t = lax.rem(grp + j, ngrp)
        pltpu.make_async_remote_copy(
            src_ref=term3,
            dst_ref=recv3.at[:, block(grp, nc2)],
            send_sem=z_sem.at[0],
            recv_sem=z_sem.at[1],
            device_id={"grp": t},
            device_id_type=MESH,
        ).start()
        return carry

    lax.fori_loop(1, ngrp, send_z, 0)

    wait_bytes(l2maps.at[pl.ds(0, ngrp - 1)], map3_sem.at[1])

    def build3(t, carry):
        ids = lax.broadcasted_iota(jnp.int32, (ng3, nc2), 0)
        onehot3[:, block(t, nc2)] = jnp.where(ids == l2maps[t][0:1], F32(1.0), F32(0.0)).astype(BF16)
        return carry

    lax.fori_loop(0, ngrp, build3, 0)
    ld_l3inv.wait()
    own3 = onehot3[:, block(grp, nc2)].astype(F32).T.astype(BF16)
    l3rows = dot(own3, l3inv[...].astype(BF16)).astype(BF16)
    q3[...] = dot(l3rows, onehot3[...]).astype(BF16)

    ld_l2inv.wait()
    res2 = dot_t(recv2[...], onehot2[...])
    local2 = fold_terms(dot_t(two_terms(res2), l2inv[...].astype(BF16)))
    local2 = two_terms(local2)

    def spread2(j, carry):
        pre[:, block(j, wide2)] = fold_terms(dot(local2, onehot2[:, block(j, wide2)]))
        return carry

    lax.fori_loop(0, nsub * nc1 // wide2, spread2, 0)

    wait_bytes(recv3.at[:, pl.ds(0, (ngrp - 1) * nc2)], z_sem.at[1])
    picked = two_terms(fold_terms(dot_t(two_terms(recv3[...]), q3[...])))

    def spread3(j, carry):
        here = block(j, wide2)
        back[:, here] = (pre[:, here] + fold_terms(dot(picked, b2[:, here]))).astype(BF16)
        return carry

    lax.fori_loop(0, nsub * nc1 // wide2, spread3, 0)

    def send_back(j, carry):
        t = lax.rem(sub + j, nsub)
        pltpu.make_async_remote_copy(
            src_ref=back.at[:, block(t, nc1)],
            dst_ref=xcoef.at[block(sub, kc), :],
            send_sem=back_sem.at[0],
            recv_sem=back_sem.at[1],
            device_id={"sub": t},
            device_id_type=MESH,
        ).start()
        return carry

    lax.fori_loop(1, nsub, send_back, 0)
    xcoef[block(sub, kc), :] = back[:, block(sub, nc1)]

    order_col = jnp.broadcast_to(order[...].astype(F32), (LANES, n_if)).T.astype(jnp.int32)

    def build_perm(b, carry):
        ids = lax.broadcasted_iota(jnp.int32, (n_if, LANES), 1) + b * LANES
        perm[:, block(b, LANES)] = jnp.where(ids == order_col, F32(1.0), F32(0.0)).astype(BF16)
        return carry

    lax.fori_loop(0, n_if // LANES, build_perm, 0)
    ld_linv.wait()

    def local(r, carry):
        rows = block(r, face)
        p = perm[rows, :]
        basis_f[rows, :] = dot(p, basis[...]).astype(BF16)
        linv_f = dot(p, linv[...]).astype(BF16)
        local_f[rows, :] = dot(linv_f, weighted[...])
        return carry

    lax.fori_loop(0, 4, local, 0)
    ld_schur.wait()

    def permute_schur(r, carry):
        rows = block(r, face)
        schur_p[rows, :] = dot(schur[rows, :], perm_t[...]).astype(BF16)
        return carry

    lax.fori_loop(0, 4, permute_schur, 0)

    wait_bytes(xcoef.at[pl.ds(0, (nsub - 1) * kc), :], back_sem.at[1])

    def face_copy(f, h):
        axis, step = (("sub", -1), ("sub", 1), ("grp", -1), ("grp", 1))[f]
        at = lax.axis_index(axis)
        size = nsub if axis == "sub" else ngrp
        other = jnp.clip(at + step, 0, size - 1)
        facing = (1, 0, 3, 2)[f]
        here = pl.ds(h * half, half)
        return pltpu.make_async_remote_copy(
            src_ref=mine.at[pl.ds(f * face, face), here],
            dst_ref=theirs.at[pl.ds(facing * face, face), here],
            send_sem=face_send.at[f, h],
            recv_sem=face_recv.at[facing, h],
            device_id={axis: other},
            device_id_type=MESH,
        )

    for h in range(2):
        here = slice(h * half, (h + 1) * half)
        for f in (2, 3, 0, 1):
            rows = slice(f * face, (f + 1) * face)
            coarse_f = dot_t(basis_f[rows, :], xcoef[here, :])
            mine[rows, here] = (weights[f][0:1, 0:1] * (local_f[rows, here] + coarse_f)).astype(BF16)

            @pl.when(exists[f])
            def _(f=f, h=h):
                face_copy(f, h).start()

            @pl.when(jnp.logical_not(exists[f]))
            def _(rows=rows, here=here):
                theirs[rows, here] = jnp.zeros((face, half), BF16)

    def arrive(f, h):
        @pl.when(exists[f])
        def _():
            wait_bytes(theirs.at[pl.ds(f * face, face), pl.ds(h * half, half)], face_recv.at[f, h])

    def summed(f, h):
        rows, here = slice(f * face, (f + 1) * face), slice(h * half, (h + 1) * half)
        return (mine[rows, here].astype(F32) + theirs[rows, here].astype(F32)).astype(BF16)

    for h in range(2):
        here = pl.ds(h * half, half)
        arrive(0, h)
        arrive(1, h)
        lower = jnp.concatenate([summed(0, h), summed(1, h)], axis=0)

        def first(r, carry, lower=lower, here=here):
            rows = block(r, face)
            sol_acc[rows, here] = dot(perm_t[rows, 0 : 2 * face], lower)
            img_acc[rows, here] = dot(schur_p[rows, 0 : 2 * face], lower)
            return carry

        lax.fori_loop(0, 4, first, 0)

    stores = []
    for h in range(2):
        here = pl.ds(h * half, half)
        arrive(2, h)
        arrive(3, h)
        upper = jnp.concatenate([summed(2, h), summed(3, h)], axis=0)

        def second(r, carry, upper=upper, here=here):
            rows = block(r, face)
            sol[rows, here] = (sol_acc[rows, here] + dot(perm_t[rows, 2 * face : 4 * face], upper)).astype(BF16)
            img[rows, here] = (img_acc[rows, here] + dot(schur_p[rows, 2 * face : 4 * face], upper)).astype(BF16)
            return carry

        lax.fori_loop(0, 4, second, 0)
        for i, (src, dst) in enumerate([(sol, sol_h), (img, img_h)]):
            store = pltpu.make_async_copy(src.at[:, here], dst.at[0, 0, :, here], out_sem.at[i, h])
            store.start()
            stores.append(store)

    wait_bytes(cmaps.at[pl.ds(0, nsub - 1)], map2_sem.at[0])
    wait_bytes(l2maps.at[pl.ds(0, ngrp - 1)], map3_sem.at[0])
    wait_bytes(cres_t.at[pl.ds(0, (nsub - 1) * kc), :], a2a_sem.at[0])
    wait_bytes(recv3.at[:, pl.ds(0, (ngrp - 1) * nc2)], z_sem.at[0])
    wait_bytes(back.at[:, pl.ds(0, (nsub - 1) * nc1)], back_sem.at[0])
    for f in range(4):

        @pl.when(exists[f])
        def _(f=f):
            for h in range(2):
                wait_bytes(mine.at[pl.ds(f * face, face), pl.ds(h * half, half)], face_send.at[f, h])

    for store in stores:
        store.wait()


def shards(nsub, ngrp, *args):
    resid, order, stiff, schur, linv, basis, cmap, l2inv, l2basis, l2map, l3inv = args
    n_if, cols = resid.shape[2:]
    nc1 = basis.shape[3]
    ng2, nc2 = l2basis.shape[1:]
    ng3 = l3inv.shape[0]
    kc = cols // nsub
    vmem = pltpu.VMEM
    dma = pltpu.SemaphoreType.DMA
    scratch = [
        vmem((n_if, cols), BF16),
        vmem((1, n_if), jnp.int32),
        pltpu.SMEM((ngrp, nsub), F32),
        vmem((n_if, n_if), BF16),
        vmem((n_if, n_if), BF16),
        vmem((n_if, nc1), BF16),
        vmem((1, nc1), jnp.int32),
        vmem((ng2, ng2), F32),
        vmem((ng2, nc2), F32),
        vmem((1, nc2), jnp.int32),
        vmem((ng3, ng3), F32),
        vmem((nsub, 8, nc1), jnp.int32),
        vmem((ngrp, 8, nc2), jnp.int32),
        vmem((n_if, 2 * LANES), BF16),
        vmem((n_if, n_if), BF16),
        vmem((n_if, n_if), BF16),
        vmem((n_if, cols), BF16),
        vmem((cols, nc1), BF16),
        vmem((kc, nsub * nc1), BF16),
        vmem((ng2, nsub * nc1), BF16),
        vmem((nc2, nsub * nc1), BF16),
        vmem((ng3, ngrp * nc2), BF16),
        vmem((nc2, ngrp * nc2), BF16),
        vmem((kc, ngrp * nc2), F32),
        vmem((kc, nc2), F32),
        vmem((kc, nsub * nc1), F32),
        vmem((kc, nsub * nc1), BF16),
        vmem((cols, nc1), BF16),
        vmem((n_if, nc1), BF16),
        vmem((n_if, cols), F32),
        vmem((n_if, n_if), BF16),
        vmem((n_if, cols), BF16),
        vmem((n_if, cols), BF16),
        vmem((n_if, cols), F32),
        vmem((n_if, cols), F32),
        vmem((n_if, cols), BF16),
        vmem((n_if, cols), BF16),
        dma((11,)),
        dma((2, 2)),
        dma((2,)),
        dma((2,)),
        dma((2,)),
        dma((2,)),
        dma((2,)),
        dma((4, 2)),
        dma((4, 2)),
    ]
    flops = 2 * n_if * cols * n_if * 3 + 4 * n_if**3
    out = jax.ShapeDtypeStruct((1, 1, n_if, cols), BF16)
    return pl.pallas_call(
        functools.partial(kernel, nsub, ngrp),
        out_shape=(out, out),
        in_specs=[pl.BlockSpec(memory_space=pl.ANY)] * 11,
        out_specs=(pl.BlockSpec(memory_space=pl.ANY),) * 2,
        scratch_shapes=scratch,
        compiler_params=pltpu.CompilerParams(
            collective_id=0, has_side_effects=True, vmem_limit_bytes=56 * 1024 * 1024
        ),
        cost_estimate=pl.CostEstimate(flops=flops, bytes_accessed=11 << 20, transcendentals=0),
        name="bddc_apply",
    )(*args)


def solution(mesh):
    placed = (
        P("grp", "sub", None, None),
        P("grp", "sub", None),
        P(),
        P("grp", "sub", None, None),
        P("grp", "sub", None, None),
        P("grp", "sub", None, None),
        P("grp", "sub", None),
        P("grp", None, None),
        P("grp", None, None),
        P("grp", None),
        P(),
    )
    return jax.shard_map(
        functools.partial(shards, mesh.shape["sub"], mesh.shape["grp"]),
        mesh=mesh,
        in_specs=placed,
        out_specs=(P("grp", "sub", None, None), P("grp", "sub", None, None)),
        check_vma=False,
    )
```

```python
import functools

import jax
import jax.numpy as jnp
from jax import lax
from jax.experimental import pallas as pl
from jax.experimental.pallas import tpu as pltpu
from jax.sharding import PartitionSpec as P

MESH = pl.DeviceIdType.MESH
F32 = jnp.float32
BF16 = jnp.bfloat16
LANES = 128


def dot(a, b):
    return jnp.dot(a, b, preferred_element_type=F32)


def dot_t(a, b):
    return lax.dot_general(a, b, (((1,), (1,)), ((), ())), preferred_element_type=F32)


def two_terms(x):
    high = x.astype(BF16)
    low = (x - high.astype(F32)).astype(BF16)
    return jnp.concatenate([high, low], axis=0)


def fold_terms(x):
    half = x.shape[0] // 2
    return x[:half] + x[half:]


def block(index, size):
    return pl.ds(pl.multiple_of(index * size, size), size)


def kernel(
    nsub,
    ngrp,
    resid_v,
    order_v,
    stiff_h,
    schur_h,
    linv_h,
    basis_v,
    cmap_v,
    l2inv_h,
    l2basis_h,
    l2map_v,
    l3inv_h,
    sol_v,
    img_v,
    stiff,
    schur,
    linv,
    l2inv,
    l2basis,
    l3inv,
    cmaps,
    l2maps,
    perm_t,
    perm,
    dofw,
    weighted,
    cres_t,
    recv2,
    onehot2,
    b2,
    onehot3,
    q3,
    recv3,
    term3,
    back,
    xcoef,
    local,
    schur_p,
    sendable,
    mine,
    theirs,
    sol_acc,
    img_acc,
    in_sem,
    map2_sem,
    map3_sem,
    a2a_sem,
    z_sem,
    back_sem,
    face_send,
    face_recv,
):
    grp = lax.axis_index("grp")
    sub = lax.axis_index("sub")
    n_if, cols = weighted.shape
    face = n_if // 4
    nc1 = xcoef.shape[1]
    ng2, nc2 = l2basis.shape
    ng3 = l3inv.shape[0]
    kc = cols // nsub
    half = cols // 2
    basis = basis_v[0, 0]
    order = order_v[0]

    loads = [
        pltpu.make_async_copy(src, dst, in_sem.at[i])
        for i, (src, dst) in enumerate(
            [
                (stiff_h, stiff),
                (l2basis_h.at[0], l2basis),
                (l2inv_h.at[0], l2inv),
                (l3inv_h, l3inv),
                (linv_h.at[0, 0], linv),
                (schur_h.at[0, 0], schur),
            ]
        )
    ]
    for load in loads:
        load.start()
    ld_stiff, ld_l2basis, ld_l2inv, ld_l3inv, ld_linv, ld_schur = loads

    barrier = pltpu.get_barrier_semaphore()

    def greet_sub(j, carry):
        pl.semaphore_signal(barrier, inc=1, device_id={"sub": lax.rem(sub + j, nsub)}, device_id_type=MESH)
        return carry

    def greet_grp(j, carry):
        pl.semaphore_signal(barrier, inc=1, device_id={"grp": lax.rem(grp + j, ngrp)}, device_id_type=MESH)
        return carry

    lax.fori_loop(1, nsub, greet_sub, 0)
    lax.fori_loop(1, ngrp, greet_grp, 0)

    cmaps[sub] = jnp.broadcast_to(cmap_v[0], (8, nc1))
    l2maps[grp] = jnp.broadcast_to(l2map_v[...], (8, nc2))
    ld_stiff.wait()
    own = stiff[grp, sub]

    def weight(g, s, present):
        other = stiff[jnp.clip(g, 0, ngrp - 1), jnp.clip(s, 0, nsub - 1)]
        num = jnp.full((8, face), own, F32)
        den = num + jnp.full((8, face), other, F32)
        here = jnp.full((8, face), present.astype(jnp.int32), jnp.int32) > 0
        return jnp.where(here, num / den, F32(1.0))[0:1]

    exists = [sub > 0, sub < nsub - 1, grp > 0, grp < ngrp - 1]
    weights = jnp.concatenate(
        [
            weight(grp, sub - 1, exists[0]),
            weight(grp, sub + 1, exists[1]),
            weight(grp - 1, sub, exists[2]),
            weight(grp + 1, sub, exists[3]),
        ],
        axis=1,
    )

    pl.semaphore_wait(barrier, nsub + ngrp - 2)

    def send_map2(j, carry):
        t = lax.rem(sub + j, nsub)
        pltpu.make_async_remote_copy(
            src_ref=cmaps.at[sub],
            dst_ref=cmaps.at[sub],
            send_sem=map2_sem.at[0],
            recv_sem=map2_sem.at[1],
            device_id={"sub": t},
            device_id_type=MESH,
        ).start()
        return carry

    def send_map3(j, carry):
        t = lax.rem(grp + j, ngrp)
        pltpu.make_async_remote_copy(
            src_ref=l2maps.at[grp],
            dst_ref=l2maps.at[grp],
            send_sem=map3_sem.at[0],
            recv_sem=map3_sem.at[1],
            device_id={"grp": t},
            device_id_type=MESH,
        ).start()
        return carry

    lax.fori_loop(1, nsub, send_map2, 0)
    lax.fori_loop(1, ngrp, send_map3, 0)

    def weigh(r, carry):
        rows = block(r, face)
        ids = lax.broadcasted_iota(jnp.int32, (face, n_if), 0) + r * face
        here = ids == order
        perm_t[rows, :] = jnp.where(here, F32(1.0), F32(0.0)).astype(BF16)
        dw = jnp.sum(jnp.where(here, weights, F32(0.0)), axis=1, keepdims=True)
        dofw[rows, :] = jnp.broadcast_to(dw, (face, LANES))
        weighted[rows, :] = (dw * resid_v[0, 0, rows, :].astype(F32)).astype(BF16)
        return carry

    lax.fori_loop(0, 4, weigh, 0)
    coarse = dot(basis.astype(F32).T.astype(BF16), weighted[...])
    cres_t[...] = coarse.T.astype(BF16)

    def send_a2a(j, carry):
        t = lax.rem(sub + j, nsub)
        pltpu.make_async_remote_copy(
            src_ref=cres_t.at[block(t, kc), :],
            dst_ref=recv2.at[:, block(sub, nc1)],
            send_sem=a2a_sem.at[0],
            recv_sem=a2a_sem.at[1],
            device_id={"sub": t},
            device_id_type=MESH,
        ).start()
        return carry

    lax.fori_loop(1, nsub, send_a2a, 0)
    recv2[:, block(sub, nc1)] = cres_t[block(sub, kc), :]

    def wait_bytes(ref, sem):
        pltpu.make_async_copy(ref, ref, sem).wait()

    wait_bytes(cmaps.at[pl.ds(0, nsub - 1)], map2_sem.at[1])

    def build2(t, carry):
        ids = lax.broadcasted_iota(jnp.int32, (ng2, nc1), 0)
        onehot2[:, block(t, nc1)] = jnp.where(ids == cmaps[t][0:1], F32(1.0), F32(0.0)).astype(BF16)
        return carry

    lax.fori_loop(0, nsub, build2, 0)

    ld_l2basis.wait()
    l2basis_t = l2basis[...].T.astype(BF16)
    wide2 = min(1024, nsub * nc1)

    def gather2(j, carry):
        b2[:, block(j, wide2)] = dot(l2basis_t, onehot2[:, block(j, wide2)]).astype(BF16)
        return carry

    lax.fori_loop(0, nsub * nc1 // wide2, gather2, 0)

    wait_bytes(recv2.at[:, pl.ds(0, (nsub - 1) * nc1)], a2a_sem.at[1])
    term3[...] = dot_t(recv2[...], b2[...])
    recv3[:, block(grp, nc2)] = term3[...]

    def send_z(j, carry):
        t = lax.rem(grp + j, ngrp)
        pltpu.make_async_remote_copy(
            src_ref=term3,
            dst_ref=recv3.at[:, block(grp, nc2)],
            send_sem=z_sem.at[0],
            recv_sem=z_sem.at[1],
            device_id={"grp": t},
            device_id_type=MESH,
        ).start()
        return carry

    lax.fori_loop(1, ngrp, send_z, 0)

    ld_l2inv.wait()
    res2 = dot_t(recv2[...], onehot2[...])
    local2 = fold_terms(dot_t(two_terms(res2), l2inv[...].astype(BF16)))
    wait_bytes(l2maps.at[pl.ds(0, ngrp - 1)], map3_sem.at[1])

    def build3(t, carry):
        ids = lax.broadcasted_iota(jnp.int32, (ng3, nc2), 0)
        onehot3[:, block(t, nc2)] = jnp.where(ids == l2maps[t][0:1], F32(1.0), F32(0.0)).astype(BF16)
        return carry

    lax.fori_loop(0, ngrp, build3, 0)
    ld_l3inv.wait()
    own3 = onehot3[:, block(grp, nc2)].astype(F32).T.astype(BF16)
    l3rows = dot(own3, l3inv[...].astype(BF16)).astype(BF16)
    q3[...] = dot(l3rows, onehot3[...]).astype(BF16)

    wait_bytes(recv3.at[:, pl.ds(0, (ngrp - 1) * nc2)], z_sem.at[1])
    picked = two_terms(fold_terms(dot_t(two_terms(recv3[...]), q3[...])))
    sol2 = (local2 + fold_terms(dot(picked, l2basis_t))).astype(BF16)

    def spread(j, carry):
        back[:, block(j, wide2)] = dot(sol2, onehot2[:, block(j, wide2)]).astype(BF16)
        return carry

    lax.fori_loop(0, nsub * nc1 // wide2, spread, 0)

    def send_back(j, carry):
        t = lax.rem(sub + j, nsub)
        pltpu.make_async_remote_copy(
            src_ref=back.at[:, block(t, nc1)],
            dst_ref=xcoef.at[block(sub, kc), :],
            send_sem=back_sem.at[0],
            recv_sem=back_sem.at[1],
            device_id={"sub": t},
            device_id_type=MESH,
        ).start()
        return carry

    lax.fori_loop(1, nsub, send_back, 0)
    xcoef[block(sub, kc), :] = back[:, block(sub, nc1)]

    ld_linv.wait()
    local[...] = dot(linv[...], weighted[...])
    order_col = jnp.broadcast_to(order.astype(F32), (LANES, n_if)).T.astype(jnp.int32)

    def build_perm(b, carry):
        ids = lax.broadcasted_iota(jnp.int32, (n_if, LANES), 1) + b * LANES
        perm[:, block(b, LANES)] = jnp.where(ids == order_col, F32(1.0), F32(0.0)).astype(BF16)
        return carry

    lax.fori_loop(0, n_if // LANES, build_perm, 0)

    def face_copy(f, h):
        axis, step = (("sub", -1), ("sub", 1), ("grp", -1), ("grp", 1))[f]
        at = lax.axis_index(axis)
        size = nsub if axis == "sub" else ngrp
        other = jnp.clip(at + step, 0, size - 1)
        facing = (1, 0, 3, 2)[f]
        here = pl.ds(h * half, half)
        return pltpu.make_async_remote_copy(
            src_ref=mine.at[pl.ds(f * face, face), here],
            dst_ref=theirs.at[pl.ds(facing * face, face), here],
            send_sem=face_send.at[f, h],
            recv_sem=face_recv.at[facing, h],
            device_id={axis: other},
            device_id_type=MESH,
        )

    wait_bytes(xcoef.at[pl.ds(0, (nsub - 1) * kc), :], back_sem.at[1])

    for h in range(2):
        here = slice(h * half, (h + 1) * half)
        coarse_part = dot_t(basis, xcoef[here, :])
        reps = -(-half // LANES)
        wide = jnp.concatenate([dofw[...]] * reps, axis=1)[:, :half]
        sendable[...] = (wide * (local[:, here] + coarse_part)).astype(BF16)
        for pair in ((2, 3), (0, 1)):
            rows = slice(pair[0] * face, (pair[1] + 1) * face)
            mine[rows, here] = dot(perm[rows, :], sendable[...]).astype(BF16)
            for f in pair:

                @pl.when(exists[f])
                def _(f=f, h=h):
                    face_copy(f, h).start()

                @pl.when(jnp.logical_not(exists[f]))
                def _(f=f, here=here):
                    theirs[f * face : (f + 1) * face, here] = jnp.zeros((face, half), BF16)

    ld_schur.wait()
    wide_p = n_if // 2

    def permute_schur(j, carry):
        schur_p[:, block(j, wide_p)] = dot(schur[...], perm_t[:, block(j, wide_p)]).astype(BF16)
        return carry

    lax.fori_loop(0, n_if // wide_p, permute_schur, 0)

    def arrive(f, h):
        @pl.when(exists[f])
        def _():
            wait_bytes(theirs.at[pl.ds(f * face, face), pl.ds(h * half, half)], face_recv.at[f, h])

    def summed(pair, h):
        rows, here = slice(pair[0] * face, (pair[1] + 1) * face), slice(h * half, (h + 1) * half)
        return (mine[rows, here].astype(F32) + theirs[rows, here].astype(F32)).astype(BF16)

    for h in range(2):
        here = slice(h * half, (h + 1) * half)
        arrive(0, h)
        arrive(1, h)
        lower = summed((0, 1), h)
        sol_acc[:, here] = dot(perm_t[:, 0 : 2 * face], lower).astype(BF16)
        img_acc[:, here] = dot(schur_p[:, 0 : 2 * face], lower)

    for h in range(2):
        here = slice(h * half, (h + 1) * half)
        arrive(2, h)
        arrive(3, h)
        upper = summed((2, 3), h)
        sol_v[0, 0, :, here] = (sol_acc[:, here].astype(F32) + dot(perm_t[:, 2 * face :], upper)).astype(BF16)
        img_v[0, 0, :, here] = (img_acc[:, here] + dot(schur_p[:, 2 * face :], upper)).astype(BF16)

    wait_bytes(cmaps.at[pl.ds(0, nsub - 1)], map2_sem.at[0])
    wait_bytes(l2maps.at[pl.ds(0, ngrp - 1)], map3_sem.at[0])
    wait_bytes(cres_t.at[pl.ds(0, (nsub - 1) * kc), :], a2a_sem.at[0])
    wait_bytes(recv3.at[:, pl.ds(0, (ngrp - 1) * nc2)], z_sem.at[0])
    wait_bytes(back.at[:, pl.ds(0, (nsub - 1) * nc1)], back_sem.at[0])
    for f in range(4):

        @pl.when(exists[f])
        def _(f=f):
            for h in range(2):
                wait_bytes(mine.at[pl.ds(f * face, face), pl.ds(h * half, half)], face_send.at[f, h])


def store(sol, img, sol_h, img_h, sem):
    copies = [pltpu.make_async_copy(sol, sol_h, sem.at[0]), pltpu.make_async_copy(img, img_h, sem.at[1])]
    for copy in copies:
        copy.start()
    for copy in copies:
        copy.wait()


def shards(nsub, ngrp, *args):
    resid, order, stiff, schur, linv, basis, cmap, l2inv, l2basis, l2map, l3inv = args
    n_if, cols = resid.shape[2:]
    nc1 = basis.shape[3]
    ng2, nc2 = l2basis.shape[1:]
    ng3 = l3inv.shape[0]
    kc = cols // nsub
    half = cols // 2
    vmem = pltpu.VMEM
    dma = pltpu.SemaphoreType.DMA
    scratch = [
        pltpu.SMEM((ngrp, nsub), F32),
        vmem((n_if, n_if), BF16),
        vmem((n_if, n_if), BF16),
        vmem((ng2, ng2), F32),
        vmem((ng2, nc2), F32),
        vmem((ng3, ng3), F32),
        vmem((nsub, 8, nc1), jnp.int32),
        vmem((ngrp, 8, nc2), jnp.int32),
        vmem((n_if, n_if), BF16),
        vmem((n_if, n_if), BF16),
        vmem((n_if, LANES), F32),
        vmem((n_if, cols), BF16),
        vmem((cols, nc1), BF16),
        vmem((kc, nsub * nc1), BF16),
        vmem((ng2, nsub * nc1), BF16),
        vmem((nc2, nsub * nc1), BF16),
        vmem((ng3, ngrp * nc2), BF16),
        vmem((nc2, ngrp * nc2), BF16),
        vmem((kc, ngrp * nc2), F32),
        vmem((kc, nc2), F32),
        vmem((kc, nsub * nc1), BF16),
        vmem((cols, nc1), BF16),
        vmem((n_if, cols), F32),
        vmem((n_if, n_if), BF16),
        vmem((n_if, half), BF16),
        vmem((n_if, cols), BF16),
        vmem((n_if, cols), BF16),
        vmem((n_if, cols), BF16),
        vmem((n_if, cols), F32),
        dma((6,)),
        dma((2,)),
        dma((2,)),
        dma((2,)),
        dma((2,)),
        dma((2,)),
        dma((4, 2)),
        dma((4, 2)),
    ]
    flops = 2 * n_if * cols * n_if * 4 + 2 * n_if**3
    out = jax.ShapeDtypeStruct((1, 1, n_if, cols), BF16)
    any_, in_vmem = pl.BlockSpec(memory_space=pl.ANY), pl.BlockSpec(memory_space=vmem)
    done = pl.pallas_call(
        functools.partial(kernel, nsub, ngrp),
        out_shape=(out, out),
        in_specs=[in_vmem, in_vmem, any_, any_, any_, in_vmem, in_vmem, any_, any_, in_vmem, any_],
        out_specs=(in_vmem, in_vmem),
        scratch_shapes=scratch,
        compiler_params=pltpu.CompilerParams(
            collective_id=0, has_side_effects=True, vmem_limit_bytes=50 * 1024 * 1024
        ),
        cost_estimate=pl.CostEstimate(flops=flops, bytes_accessed=11 << 20, transcendentals=0),
        name="bddc_apply",
    )(*args)
    return pl.pallas_call(
        store,
        out_shape=(out, out),
        in_specs=[any_, any_],
        out_specs=(any_, any_),
        scratch_shapes=[dma((2,))],
        name="store",
    )(*done)


def solution(mesh):
    placed = (
        P("grp", "sub", None, None),
        P("grp", "sub", None),
        P(),
        P("grp", "sub", None, None),
        P("grp", "sub", None, None),
        P("grp", "sub", None, None),
        P("grp", "sub", None),
        P("grp", None, None),
        P("grp", None, None),
        P("grp", None),
        P(),
    )
    return jax.shard_map(
        functools.partial(shards, mesh.shape["sub"], mesh.shape["grp"]),
        mesh=mesh,
        in_specs=placed,
        out_specs=(P("grp", "sub", None, None), P("grp", "sub", None, None)),
        check_vma=False,
    )
```

```python
import functools

import jax
import jax.numpy as jnp
from jax import lax
from jax.experimental import pallas as pl
from jax.experimental.pallas import tpu as pltpu
from jax.sharding import PartitionSpec as P

MESH = pl.DeviceIdType.MESH
F32 = jnp.float32
BF16 = jnp.bfloat16
LANES = 128


def dot(a, b):
    return jnp.dot(a, b, preferred_element_type=F32)


def dot_t(a, b):
    return lax.dot_general(a, b, (((1,), (1,)), ((), ())), preferred_element_type=F32)


def two_terms(x):
    high = x.astype(BF16)
    low = (x - high.astype(F32)).astype(BF16)
    return jnp.concatenate([high, low], axis=0)


def fold_terms(x):
    half = x.shape[0] // 2
    return x[:half] + x[half:]


def block(index, size):
    return pl.ds(pl.multiple_of(index * size, size), size)


def far_first(r):
    return r + lax.div(r, 2) - 2 * lax.div(r, 3)


def kernel(
    nsub,
    ngrp,
    resid_h,
    order_h,
    stiff_h,
    schur_h,
    linv_h,
    basis_h,
    cmap_h,
    l2inv_h,
    l2basis_h,
    l2map_h,
    l3inv_h,
    sol_h,
    img_h,
    resid,
    order_s,
    basis_s,
    cmap,
    l2map,
    stiff,
    schur,
    linv,
    l2inv,
    l2basis,
    l3inv,
    l2maps,
    perm_t,
    perm,
    dofw,
    weighted,
    t_src,
    t_recv,
    c_src,
    c_recv,
    recv2,
    onehot2,
    onehot3,
    q3,
    recv3,
    term3,
    back,
    xcoef,
    xn,
    scaled,
    mine_l,
    theirs_l,
    basis_f,
    basis_n,
    schur_p,
    mine,
    sol_acc,
    img_acc,
    sol,
    img,
    in_sem,
    out_sem,
    map3_sem,
    t_sem,
    c_sem,
    z_sem,
    back_sem,
    lf_send,
    lf_recv,
    bf_send,
    bf_recv,
    xf_send,
    xf_recv,
):
    grp = lax.axis_index("grp")
    sub = lax.axis_index("sub")
    n_if, cols = weighted.shape
    face = n_if // 4
    nc1 = xcoef.shape[1]
    ng2, nc2 = l2basis.shape
    ng3 = l3inv.shape[0]
    kc = cols // nsub
    half = cols // 2

    loads = [
        pltpu.make_async_copy(src, dst, in_sem.at[i])
        for i, (src, dst) in enumerate(
            [
                (order_h.at[0], order_s),
                (stiff_h, stiff),
                (cmap_h.at[0], cmap),
                (l2map_h, l2map),
                (resid_h.at[0, 0], resid),
                (basis_h.at[0, 0], basis_s),
                (l2basis_h.at[0], l2basis),
                (linv_h.at[0, 0], linv),
                (l2inv_h.at[0], l2inv),
                (l3inv_h, l3inv),
                (schur_h.at[0, 0], schur),
            ]
        )
    ]
    for load in loads[:8]:
        load.start()
    ld_order, ld_stiff, ld_cmap, ld_l2map, ld_resid, ld_basis, ld_l2basis, ld_linv, ld_l2inv, ld_l3inv, ld_schur = loads

    nx = 4 if nsub % 8 == 0 else 2
    ny = nsub // (2 * nx)
    at_y, at_x, at_c = lax.div(sub, 2 * nx), lax.rem(lax.div(sub, 2), nx), lax.rem(sub, 2)

    def peer_sub(i):
        j = nsub - 1 - i
        y = lax.rem(at_y + far_first(lax.div(j, 2 * nx)), ny)
        x = lax.rem(at_x + far_first(lax.rem(lax.div(j, 2), nx)), nx)
        return (y * nx + x) * 2 + lax.rem(at_c + lax.rem(j, 2), 2)

    def peer_grp(i):
        off = ngrp // 2 + lax.div(i + 1, 2) * (1 - 2 * lax.rem(i, 2))
        return lax.rem(grp + off, ngrp)

    barrier = pltpu.get_barrier_semaphore()

    def greet_sub(i, carry):
        pl.semaphore_signal(barrier, inc=1, device_id={"sub": peer_sub(i)}, device_id_type=MESH)
        return carry

    def greet_grp(i, carry):
        pl.semaphore_signal(barrier, inc=1, device_id={"grp": peer_grp(i)}, device_id_type=MESH)
        return carry

    lax.fori_loop(0, nsub - 1, greet_sub, 0)
    lax.fori_loop(0, ngrp - 1, greet_grp, 0)

    ld_stiff.wait()
    own = stiff[grp, sub]
    exists = [sub > 0, sub < nsub - 1, grp > 0, grp < ngrp - 1]
    weights, their_weights = [], []
    for f, (g, s) in enumerate(((grp, sub - 1), (grp, sub + 1), (grp - 1, sub), (grp + 1, sub))):
        other = stiff[jnp.clip(g, 0, ngrp - 1), jnp.clip(s, 0, nsub - 1)]
        here = jnp.full((8, face), exists[f].astype(jnp.int32), jnp.int32) > 0
        num, nbr = jnp.full((8, face), own, F32), jnp.full((8, face), other, F32)
        weights.append(jnp.where(here, num / (num + nbr), F32(1.0))[0:1])
        their_weights.append((nbr / (nbr + num))[0:1])
    all_weights = jnp.concatenate(weights, axis=1)

    for f in range(4):

        @pl.when(jnp.logical_not(exists[f]))
        def _(f=f):
            rows = slice(f * face, (f + 1) * face)
            theirs_l[rows, :] = jnp.zeros((face, cols), BF16)
            basis_n[rows, :] = jnp.zeros((face, nc1), BF16)
            xn[f] = jnp.zeros((cols, nc1), BF16)

    ld_cmap.wait()
    ld_l2map.wait()
    l2maps[grp] = jnp.broadcast_to(l2map[...], (8, nc2))
    ld_order.wait()
    order = order_s[...]
    ld_resid.wait()
    ld_basis.wait()
    basis = basis_s[...]

    def weigh(r, carry):
        rows = block(r, face)
        ids = lax.broadcasted_iota(jnp.int32, (face, n_if), 0) + r * face
        here = ids == order
        perm_t[rows, :] = jnp.where(here, F32(1.0), F32(0.0)).astype(BF16)
        dw = jnp.sum(jnp.where(here, all_weights, F32(0.0)), axis=1, keepdims=True)
        dofw[rows, :] = jnp.broadcast_to(dw, (face, LANES))
        weighted[rows, :] = (dw * resid[rows, :].astype(F32)).astype(BF16)
        return carry

    lax.fori_loop(0, 4, weigh, 0)
    coarse = dot(basis.astype(F32).T.astype(BF16), weighted[...])
    cres_t = coarse.T.astype(BF16)
    ld_l2basis.wait()
    l2basis_t = l2basis[...].T.astype(BF16)
    own_ids = lax.broadcasted_iota(jnp.int32, (ng2, nc1), 0)
    own_map = jnp.where(own_ids == cmap[...], F32(1.0), F32(0.0)).astype(BF16)
    own_rows = dot(l2basis_t, own_map).astype(BF16)
    t_src[...] = dot_t(cres_t, own_rows).astype(BF16).reshape(nsub, kc, nc2)
    c_src[:, 0:kc, :] = cres_t.reshape(nsub, kc, nc1)
    high = lax.shift_right_logical(cmap[...], 8)
    map_rows = jnp.concatenate(
        [high.astype(F32), (cmap[...] - high * 256).astype(F32), jnp.zeros((kc - 2, nc1), F32)], axis=0
    ).astype(BF16)
    c_src[:, kc : 2 * kc, :] = jnp.broadcast_to(map_rows[None], (nsub, kc, nc1))

    for load in loads[8:]:
        load.start()

    ld_linv.wait()
    wide = jnp.concatenate([dofw[...]] * (-(-cols // LANES)), axis=1)[:, :cols]
    scaled[...] = (wide * dot(linv[...], weighted[...])).astype(BF16)
    order_col = jnp.broadcast_to(order.astype(F32), (LANES, n_if)).T.astype(jnp.int32)

    def build_perm(b, carry):
        ids = lax.broadcasted_iota(jnp.int32, (n_if, LANES), 1) + b * LANES
        perm[:, block(b, LANES)] = jnp.where(ids == order_col, F32(1.0), F32(0.0)).astype(BF16)
        return carry

    lax.fori_loop(0, n_if // LANES, build_perm, 0)

    pl.semaphore_wait(barrier, nsub + ngrp - 2)

    def wait_bytes(ref, sem):
        pltpu.make_async_copy(ref, ref, sem).wait()

    def send_t(i, carry):
        t = peer_sub(i)
        pltpu.make_async_remote_copy(
            src_ref=t_src.at[t],
            dst_ref=t_recv.at[sub],
            send_sem=t_sem.at[0],
            recv_sem=t_sem.at[1],
            device_id={"sub": t},
            device_id_type=MESH,
        ).start()
        return carry

    def send_c(i, carry):
        t = peer_sub(i)
        pltpu.make_async_remote_copy(
            src_ref=c_src.at[t],
            dst_ref=c_recv.at[sub],
            send_sem=c_sem.at[0],
            recv_sem=c_sem.at[1],
            device_id={"sub": t},
            device_id_type=MESH,
        ).start()
        return carry

    def send_map3(i, carry):
        pltpu.make_async_remote_copy(
            src_ref=l2maps.at[grp],
            dst_ref=l2maps.at[grp],
            send_sem=map3_sem.at[0],
            recv_sem=map3_sem.at[1],
            device_id={"grp": peer_grp(i)},
            device_id_type=MESH,
        ).start()
        return carry

    lax.fori_loop(0, nsub - 1, send_t, 0)
    lax.fori_loop(0, nsub - 1, send_c, 0)
    lax.fori_loop(0, ngrp - 1, send_map3, 0)
    t_recv[sub] = t_src[sub]
    c_recv[sub] = c_src[sub]

    wait_bytes(t_recv.at[pl.ds(0, nsub - 1)], t_sem.at[1])
    term3[...] = jnp.sum(t_recv[...].astype(F32), axis=0)
    recv3[:, block(grp, nc2)] = term3[...]

    def send_z(i, carry):
        pltpu.make_async_remote_copy(
            src_ref=term3,
            dst_ref=recv3.at[:, block(grp, nc2)],
            send_sem=z_sem.at[0],
            recv_sem=z_sem.at[1],
            device_id={"grp": peer_grp(i)},
            device_id_type=MESH,
        ).start()
        return carry

    lax.fori_loop(0, ngrp - 1, send_z, 0)

    mine_l[...] = dot(perm[...], scaled[...]).astype(BF16)
    basis_f[...] = dot(perm[...], basis).astype(BF16)
    facing = (1, 0, 3, 2)

    def to_neighbour(f, src, dst, send_sem, recv_sem):
        axis, step = (("sub", -1), ("sub", 1), ("grp", -1), ("grp", 1))[f]
        size = nsub if axis == "sub" else ngrp
        return pltpu.make_async_remote_copy(
            src_ref=src,
            dst_ref=dst,
            send_sem=send_sem,
            recv_sem=recv_sem,
            device_id={axis: jnp.clip(lax.axis_index(axis) + step, 0, size - 1)},
            device_id_type=MESH,
        )

    for f in (2, 3, 0, 1):

        @pl.when(exists[f])
        def _(f=f):
            o = facing[f]
            rows, there = pl.ds(f * face, face), pl.ds(o * face, face)
            to_neighbour(f, mine_l.at[rows], theirs_l.at[there], lf_send.at[f], lf_recv.at[o]).start()
            to_neighbour(f, basis_f.at[rows], basis_n.at[there], bf_send.at[f], bf_recv.at[o]).start()

    wait_bytes(c_recv.at[pl.ds(0, nsub - 1)], c_sem.at[1])

    def build2(t, carry):
        recv2[:, block(t, nc1)] = c_recv[t, 0:kc, :]
        parts = c_recv[t, kc : 2 * kc, :].astype(F32)
        ids = lax.broadcasted_iota(jnp.int32, (ng2, nc1), 0)
        member = (parts[0:1] * 256.0 + parts[1:2]).astype(jnp.int32)
        onehot2[:, block(t, nc1)] = jnp.where(ids == member, F32(1.0), F32(0.0)).astype(BF16)
        return carry

    lax.fori_loop(0, nsub, build2, 0)
    ld_l2inv.wait()
    res2 = dot_t(recv2[...], onehot2[...])
    local2 = fold_terms(dot_t(two_terms(res2), l2inv[...].astype(BF16)))
    wait_bytes(l2maps.at[pl.ds(0, ngrp - 1)], map3_sem.at[1])

    def build3(t, carry):
        ids = lax.broadcasted_iota(jnp.int32, (ng3, nc2), 0)
        onehot3[:, block(t, nc2)] = jnp.where(ids == l2maps[t][0:1], F32(1.0), F32(0.0)).astype(BF16)
        return carry

    lax.fori_loop(0, ngrp, build3, 0)
    ld_l3inv.wait()
    own3 = onehot3[:, block(grp, nc2)].astype(F32).T.astype(BF16)
    l3rows = dot(own3, l3inv[...].astype(BF16)).astype(BF16)
    q3[...] = dot(l3rows, onehot3[...]).astype(BF16)

    wait_bytes(recv3.at[:, pl.ds(0, (ngrp - 1) * nc2)], z_sem.at[1])
    picked = two_terms(fold_terms(dot_t(two_terms(recv3[...]), q3[...])))
    sol2 = (local2 + fold_terms(dot(picked, l2basis_t))).astype(BF16)
    wide2 = min(1024, nsub * nc1)

    def spread(j, carry):
        back[:, block(j, wide2)] = dot(sol2, onehot2[:, block(j, wide2)]).astype(BF16)
        return carry

    lax.fori_loop(0, nsub * nc1 // wide2, spread, 0)

    def send_back(i, carry):
        t = peer_sub(i)
        pltpu.make_async_remote_copy(
            src_ref=back.at[:, block(t, nc1)],
            dst_ref=xcoef.at[block(sub, kc), :],
            send_sem=back_sem.at[0],
            recv_sem=back_sem.at[1],
            device_id={"sub": t},
            device_id_type=MESH,
        ).start()
        return carry

    lax.fori_loop(0, nsub - 1, send_back, 0)
    xcoef[block(sub, kc), :] = back[:, block(sub, nc1)]

    ld_schur.wait()
    wide_p = n_if // 2

    def permute_schur(j, carry):
        schur_p[:, block(j, wide_p)] = dot(schur[...], perm_t[:, block(j, wide_p)]).astype(BF16)
        return carry

    lax.fori_loop(0, n_if // wide_p, permute_schur, 0)

    wait_bytes(xcoef.at[pl.ds(0, (nsub - 1) * kc), :], back_sem.at[1])
    for h in range(2):
        part = pl.ds(h * half, half)
        for f in (2, 3, 0, 1):

            @pl.when(exists[f])
            def _(f=f, h=h, part=part):
                o = facing[f]
                to_neighbour(f, xcoef.at[part], xn.at[o, part], xf_send.at[f, h], xf_recv.at[o, h]).start()

    coarse_part = dot_t(basis_f[...], xcoef[...])
    for f in range(4):
        rows = slice(f * face, (f + 1) * face)
        mine[rows, :] = (mine_l[rows, :].astype(F32) + weights[f][:, 0:1] * coarse_part[rows]).astype(BF16)

    def received(f, h):
        @pl.when(exists[f])
        def _():
            wait_bytes(xn.at[f, pl.ds(h * half, half)], xf_recv.at[f, h])
            if h == 0:
                wait_bytes(theirs_l.at[pl.ds(f * face, face)], lf_recv.at[f])
                wait_bytes(basis_n.at[pl.ds(f * face, face)], bf_recv.at[f])

        rows, here = slice(f * face, (f + 1) * face), slice(h * half, (h + 1) * half)
        part = dot_t(basis_n[rows, :], xn[f, here, :])
        theirs = (theirs_l[rows, here].astype(F32) + their_weights[f][:, 0:1] * part).astype(BF16)
        return (mine[rows, here].astype(F32) + theirs.astype(F32)).astype(BF16)

    for h in range(2):
        here = slice(h * half, (h + 1) * half)
        lower = jnp.concatenate([received(0, h), received(1, h)], axis=0)
        sol_acc[:, here] = dot(perm_t[:, 0 : 2 * face], lower).astype(BF16)
        img_acc[:, here] = dot(schur_p[:, 0 : 2 * face], lower)

    stores = []
    for h in range(2):
        here = slice(h * half, (h + 1) * half)
        upper = jnp.concatenate([received(2, h), received(3, h)], axis=0)
        sol[:, here] = (sol_acc[:, here].astype(F32) + dot(perm_t[:, 2 * face :], upper)).astype(BF16)
        img[:, here] = (img_acc[:, here] + dot(schur_p[:, 2 * face :], upper)).astype(BF16)
        for i, (src, dst) in enumerate([(sol, sol_h), (img, img_h)]):
            there = pl.ds(h * half, half)
            done = pltpu.make_async_copy(src.at[:, there], dst.at[0, 0, :, there], out_sem.at[i, h])
            done.start()
            stores.append(done)

    wait_bytes(t_src.at[pl.ds(0, nsub - 1)], t_sem.at[0])
    wait_bytes(c_src.at[pl.ds(0, nsub - 1)], c_sem.at[0])
    wait_bytes(l2maps.at[pl.ds(0, ngrp - 1)], map3_sem.at[0])
    wait_bytes(recv3.at[:, pl.ds(0, (ngrp - 1) * nc2)], z_sem.at[0])
    wait_bytes(back.at[:, pl.ds(0, (nsub - 1) * nc1)], back_sem.at[0])
    for f in range(4):

        @pl.when(exists[f])
        def _(f=f):
            rows = pl.ds(f * face, face)
            wait_bytes(mine_l.at[rows], lf_send.at[f])
            wait_bytes(basis_f.at[rows], bf_send.at[f])
            for h in range(2):
                wait_bytes(xcoef.at[pl.ds(h * half, half)], xf_send.at[f, h])

    for done in stores:
        done.wait()


def store(parts, sol, img, sol_h, img_h, sol_v, img_v, in_sem, out_sem):
    size = sol_v.shape[0] // parts
    moves = []
    for i in range(parts):
        rows = pl.ds(i * size, size)
        for j, (src, via, dst) in enumerate([(sol, sol_v, sol_h), (img, img_v, img_h)]):
            load = pltpu.make_async_copy(src.at[0, 0, rows], via.at[rows], in_sem.at[j, i])
            moves.append((load, pltpu.make_async_copy(via.at[rows], dst.at[0, 0, rows], out_sem.at[j, i])))
            load.start()
    for load, save in moves:
        load.wait()
        save.start()
    for load, save in moves:
        save.wait()


def shards(nsub, ngrp, *args):
    resid, order, stiff, schur, linv, basis, cmap, l2inv, l2basis, l2map, l3inv = args
    n_if, cols = resid.shape[2:]
    nc1 = basis.shape[3]
    ng2, nc2 = l2basis.shape[1:]
    ng3 = l3inv.shape[0]
    kc = cols // nsub
    vmem = pltpu.VMEM
    dma = pltpu.SemaphoreType.DMA
    scratch = [
        vmem((n_if, cols), BF16),
        vmem((1, n_if), jnp.int32),
        vmem((n_if, nc1), BF16),
        vmem((1, nc1), jnp.int32),
        vmem((1, nc2), jnp.int32),
        pltpu.SMEM((ngrp, nsub), F32),
        vmem((n_if, n_if), BF16),
        vmem((n_if, n_if), BF16),
        vmem((ng2, ng2), F32),
        vmem((ng2, nc2), F32),
        vmem((ng3, ng3), F32),
        vmem((ngrp, 8, nc2), jnp.int32),
        vmem((n_if, n_if), BF16),
        vmem((n_if, n_if), BF16),
        vmem((n_if, LANES), F32),
        vmem((n_if, cols), BF16),
        vmem((nsub, kc, nc2), BF16),
        vmem((nsub, kc, nc2), BF16),
        vmem((nsub, 2 * kc, nc1), BF16),
        vmem((nsub, 2 * kc, nc1), BF16),
        vmem((kc, nsub * nc1), BF16),
        vmem((ng2, nsub * nc1), BF16),
        vmem((ng3, ngrp * nc2), BF16),
        vmem((nc2, ngrp * nc2), BF16),
        vmem((kc, ngrp * nc2), F32),
        vmem((kc, nc2), F32),
        vmem((kc, nsub * nc1), BF16),
        vmem((cols, nc1), BF16),
        vmem((4, cols, nc1), BF16),
        vmem((n_if, cols), BF16),
        vmem((n_if, cols), BF16),
        vmem((n_if, cols), BF16),
        vmem((n_if, nc1), BF16),
        vmem((n_if, nc1), BF16),
        vmem((n_if, n_if), BF16),
        vmem((n_if, cols), BF16),
        vmem((n_if, cols), BF16),
        vmem((n_if, cols), F32),
        vmem((n_if, cols), BF16),
        vmem((n_if, cols), BF16),
        dma((11,)),
        dma((2, 2)),
        dma((2,)),
        dma((2,)),
        dma((2,)),
        dma((2,)),
        dma((2,)),
        dma((4,)),
        dma((4,)),
        dma((4,)),
        dma((4,)),
        dma((4, 2)),
        dma((4, 2)),
    ]
    flops = 2 * n_if * cols * n_if * 4 + 2 * n_if**3
    out = jax.ShapeDtypeStruct((1, 1, n_if, cols), BF16)
    any_ = pl.BlockSpec(memory_space=pl.ANY)
    done = pl.pallas_call(
        functools.partial(kernel, nsub, ngrp),
        out_shape=(out, out),
        in_specs=[any_] * 11,
        out_specs=(any_, any_),
        scratch_shapes=scratch,
        compiler_params=pltpu.CompilerParams(
            collective_id=0, has_side_effects=True, vmem_limit_bytes=60 * 1024 * 1024
        ),
        cost_estimate=pl.CostEstimate(flops=flops, bytes_accessed=11 << 20, transcendentals=0),
        name="bddc_apply",
    )(*args)
    return pl.pallas_call(
        functools.partial(store, 4),
        out_shape=(out, out),
        in_specs=[any_, any_],
        out_specs=(any_, any_),
        scratch_shapes=[vmem((n_if, cols), BF16), vmem((n_if, cols), BF16), dma((2, 4)), dma((2, 4))],
        compiler_params=pltpu.CompilerParams(vmem_limit_bytes=60 * 1024 * 1024),
        name="store",
    )(*done)


def solution(mesh):
    placed = (
        P("grp", "sub", None, None),
        P("grp", "sub", None),
        P(),
        P("grp", "sub", None, None),
        P("grp", "sub", None, None),
        P("grp", "sub", None, None),
        P("grp", "sub", None),
        P("grp", None, None),
        P("grp", None, None),
        P("grp", None),
        P(),
    )
    return jax.shard_map(
        functools.partial(shards, mesh.shape["sub"], mesh.shape["grp"]),
        mesh=mesh,
        in_specs=placed,
        out_specs=(P("grp", "sub", None, None), P("grp", "sub", None, None)),
        check_vma=False,
    )
```

```python
import functools

import jax
import jax.numpy as jnp
from jax import lax
from jax.experimental import pallas as pl
from jax.experimental.pallas import tpu as pltpu
from jax.sharding import PartitionSpec as P

MESH = pl.DeviceIdType.MESH
F32 = jnp.float32
BF16 = jnp.bfloat16
LANES = 128


def dot(a, b):
    return jnp.dot(a, b, preferred_element_type=F32)


def dot_t(a, b):
    return lax.dot_general(a, b, (((1,), (1,)), ((), ())), preferred_element_type=F32)


def two_terms(x):
    high = x.astype(BF16)
    low = (x - high.astype(F32)).astype(BF16)
    return jnp.concatenate([high, low], axis=0)


def fold_terms(x):
    half = x.shape[0] // 2
    return x[:half] + x[half:]


def block(index, size):
    return pl.ds(pl.multiple_of(index * size, size), size)


def plane(nsub):
    nx = 4 if nsub % 8 == 0 else 2
    return nx, nsub // (2 * nx)


def far_first(r):
    return r + lax.div(r, 2) - 2 * lax.div(r, 3)


def kernel(
    nsub,
    ngrp,
    resid_h,
    order_h,
    stiff_h,
    schur_h,
    linv_h,
    basis_h,
    cmap_h,
    l2inv_h,
    l2basis_h,
    l2map_h,
    l3inv_h,
    sol_h,
    img_h,
    resid,
    order_s,
    basis_s,
    cmap,
    l2map,
    stiff,
    schur,
    linv,
    l2inv,
    l2basis,
    l3inv,
    l2maps,
    perm_t,
    perm,
    dofw,
    weighted,
    t_src,
    t_recv,
    c_src,
    c_recv,
    recv2,
    onehot2,
    onehot3,
    q3,
    recv3,
    term3,
    back,
    xtwo,
    xcoef,
    xn,
    scaled,
    mine_l,
    theirs_l,
    basis_f,
    basis_n,
    schur_p,
    base,
    pair,
    sol_acc,
    img_acc,
    sol,
    img,
    in_sem,
    out_sem,
    map3_sem,
    t_sem,
    c_sem,
    z_sem,
    back_sem,
    lf_send,
    lf_recv,
    bf_send,
    bf_recv,
    xf_send,
    xf_recv,
    xz_send,
    xz_recv,
):
    grp = lax.axis_index("grp")
    sub = lax.axis_index("sub")
    n_if, cols = weighted.shape
    face = n_if // 4
    nc1 = xcoef.shape[1]
    ng2, nc2 = l2basis.shape
    ng3 = l3inv.shape[0]
    kc = cols // nsub
    half = cols // 2

    loads = [
        pltpu.make_async_copy(src, dst, in_sem.at[i])
        for i, (src, dst) in enumerate(
            [
                (order_h.at[0], order_s),
                (stiff_h, stiff),
                (cmap_h.at[0], cmap),
                (l2map_h, l2map),
                (resid_h.at[0, 0], resid),
                (basis_h.at[0, 0], basis_s),
                (l2basis_h.at[0], l2basis),
                (linv_h.at[0, 0], linv),
                (l2inv_h.at[0], l2inv),
                (l3inv_h, l3inv),
                (schur_h.at[0, 0], schur),
            ]
        )
    ]
    for load in loads[:8]:
        load.start()
    ld_order, ld_stiff, ld_cmap, ld_l2map, ld_resid, ld_basis, ld_l2basis, ld_linv, ld_l2inv, ld_l3inv, ld_schur = loads

    nx, ny = plane(nsub)
    at_y, at_x, at_c = lax.div(sub, 2 * nx), lax.rem(lax.div(sub, 2), nx), lax.rem(sub, 2)

    def peer_sub(i):
        j = nsub - 1 - i
        y = lax.rem(at_y + far_first(lax.div(j, 2 * nx)), ny)
        x = lax.rem(at_x + far_first(lax.rem(lax.div(j, 2), nx)), nx)
        return (y * nx + x) * 2 + lax.rem(at_c + lax.rem(j, 2), 2)

    def peer_grp(i):
        off = ngrp // 2 + lax.div(i + 1, 2) * (1 - 2 * lax.rem(i, 2))
        return lax.rem(grp + off, ngrp)

    barrier = pltpu.get_barrier_semaphore()

    def greet_sub(i, carry):
        pl.semaphore_signal(barrier, inc=1, device_id={"sub": peer_sub(i)}, device_id_type=MESH)
        return carry

    def greet_grp(i, carry):
        pl.semaphore_signal(barrier, inc=1, device_id={"grp": peer_grp(i)}, device_id_type=MESH)
        return carry

    lax.fori_loop(0, nsub - 1, greet_sub, 0)
    lax.fori_loop(0, ngrp - 1, greet_grp, 0)

    ld_stiff.wait()
    own = stiff[grp, sub]
    exists = [sub > 0, sub < nsub - 1, grp > 0, grp < ngrp - 1]
    weights, their_weights = [], []
    for f, (g, s) in enumerate(((grp, sub - 1), (grp, sub + 1), (grp - 1, sub), (grp + 1, sub))):
        other = stiff[jnp.clip(g, 0, ngrp - 1), jnp.clip(s, 0, nsub - 1)]
        here = jnp.full((8, face), exists[f].astype(jnp.int32), jnp.int32) > 0
        num, nbr = jnp.full((8, face), own, F32), jnp.full((8, face), other, F32)
        weights.append(jnp.where(here, num / (num + nbr), F32(1.0))[0:1])
        their_weights.append((nbr / (nbr + num))[0:1])
    all_weights = jnp.concatenate(weights, axis=1)

    onehot2[:, 0:nc1] = jnp.zeros((ng2, nc1), BF16)
    onehot2[:, (nsub + 1) * nc1 :] = jnp.zeros((ng2, nc1), BF16)
    for f in range(4):

        @pl.when(jnp.logical_not(exists[f]))
        def _(f=f):
            rows = slice(f * face, (f + 1) * face)
            theirs_l[rows, :] = jnp.zeros((face, cols), BF16)
            basis_n[rows, :] = jnp.zeros((face, nc1), BF16)
            xn[f] = jnp.zeros((cols, nc1), BF16)

    ld_cmap.wait()
    ld_l2map.wait()
    l2maps[grp] = jnp.broadcast_to(l2map[...], (8, nc2))
    ld_order.wait()
    order = order_s[...]
    ld_resid.wait()
    ld_basis.wait()
    basis = basis_s[...]

    def weigh(r, carry):
        rows = block(r, face)
        ids = lax.broadcasted_iota(jnp.int32, (face, n_if), 0) + r * face
        here = ids == order
        perm_t[rows, :] = jnp.where(here, F32(1.0), F32(0.0)).astype(BF16)
        dw = jnp.sum(jnp.where(here, all_weights, F32(0.0)), axis=1, keepdims=True)
        dofw[rows, :] = jnp.broadcast_to(dw, (face, LANES))
        weighted[rows, :] = (dw * resid[rows, :].astype(F32)).astype(BF16)
        return carry

    lax.fori_loop(0, 4, weigh, 0)
    coarse = dot(basis.astype(F32).T.astype(BF16), weighted[...])
    cres_t = coarse.T.astype(BF16)
    ld_l2basis.wait()
    l2basis_t = l2basis[...].T.astype(BF16)
    own_ids = lax.broadcasted_iota(jnp.int32, (ng2, nc1), 0)
    own_map = jnp.where(own_ids == cmap[...], F32(1.0), F32(0.0)).astype(BF16)
    own_rows = dot(l2basis_t, own_map).astype(BF16)
    t_src[...] = dot_t(cres_t, own_rows).astype(BF16).reshape(nsub, kc, nc2)
    c_src[:, 0:kc, :] = cres_t.reshape(nsub, kc, nc1)
    high = lax.shift_right_logical(cmap[...], 8)
    map_rows = jnp.concatenate(
        [high.astype(F32), (cmap[...] - high * 256).astype(F32), jnp.zeros((kc - 2, nc1), F32)], axis=0
    ).astype(BF16)
    c_src[:, kc : 2 * kc, :] = jnp.broadcast_to(map_rows[None], (nsub, kc, nc1))

    for load in loads[8:]:
        load.start()

    pl.semaphore_wait(barrier, nsub + ngrp - 2)

    def wait_bytes(ref, sem):
        pltpu.make_async_copy(ref, ref, sem).wait()

    def send_t(i, carry):
        t = peer_sub(i)
        pltpu.make_async_remote_copy(
            src_ref=t_src.at[t],
            dst_ref=t_recv.at[sub],
            send_sem=t_sem.at[0],
            recv_sem=t_sem.at[1],
            device_id={"sub": t},
            device_id_type=MESH,
        ).start()
        return carry

    def send_c(i, carry):
        t = peer_sub(i)
        pltpu.make_async_remote_copy(
            src_ref=c_src.at[t],
            dst_ref=c_recv.at[sub],
            send_sem=c_sem.at[0],
            recv_sem=c_sem.at[1],
            device_id={"sub": t},
            device_id_type=MESH,
        ).start()
        return carry

    def send_map3(i, carry):
        pltpu.make_async_remote_copy(
            src_ref=l2maps.at[grp],
            dst_ref=l2maps.at[grp],
            send_sem=map3_sem.at[0],
            recv_sem=map3_sem.at[1],
            device_id={"grp": peer_grp(i)},
            device_id_type=MESH,
        ).start()
        return carry

    lax.fori_loop(0, nsub - 1, send_t, 0)
    lax.fori_loop(0, ngrp - 1, send_map3, 0)
    lax.fori_loop(0, nsub - 1, send_c, 0)
    t_recv[sub] = t_src[sub]
    c_recv[sub] = c_src[sub]

    ld_linv.wait()
    wide = jnp.concatenate([dofw[...]] * (-(-cols // LANES)), axis=1)[:, :cols]
    scaled[...] = (wide * dot(linv[...], weighted[...])).astype(BF16)
    order_col = jnp.broadcast_to(order.astype(F32), (LANES, n_if)).T.astype(jnp.int32)

    def build_perm(b, carry):
        ids = lax.broadcasted_iota(jnp.int32, (n_if, LANES), 1) + b * LANES
        perm[:, block(b, LANES)] = jnp.where(ids == order_col, F32(1.0), F32(0.0)).astype(BF16)
        return carry

    lax.fori_loop(0, n_if // LANES, build_perm, 0)

    wait_bytes(t_recv.at[pl.ds(0, nsub - 1)], t_sem.at[1])
    term3[...] = jnp.sum(t_recv[...].astype(F32), axis=0)
    recv3[:, block(grp, nc2)] = term3[...]

    def send_z(i, carry):
        pltpu.make_async_remote_copy(
            src_ref=term3,
            dst_ref=recv3.at[:, block(grp, nc2)],
            send_sem=z_sem.at[0],
            recv_sem=z_sem.at[1],
            device_id={"grp": peer_grp(i)},
            device_id_type=MESH,
        ).start()
        return carry

    lax.fori_loop(0, ngrp - 1, send_z, 0)

    mine_l[...] = dot(perm[...], scaled[...]).astype(BF16)
    basis_f[...] = dot(perm[...], basis).astype(BF16)
    facing = (1, 0, 3, 2)

    def to_neighbour(f, src, dst, send_sem, recv_sem):
        axis, step = (("sub", -1), ("sub", 1), ("grp", -1), ("grp", 1))[f]
        size = nsub if axis == "sub" else ngrp
        return pltpu.make_async_remote_copy(
            src_ref=src,
            dst_ref=dst,
            send_sem=send_sem,
            recv_sem=recv_sem,
            device_id={axis: jnp.clip(lax.axis_index(axis) + step, 0, size - 1)},
            device_id_type=MESH,
        )

    for f in (2, 3, 0, 1):

        @pl.when(exists[f])
        def _(f=f):
            o = facing[f]
            rows, there = pl.ds(f * face, face), pl.ds(o * face, face)
            to_neighbour(f, mine_l.at[rows], theirs_l.at[there], lf_send.at[f], lf_recv.at[o]).start()
            to_neighbour(f, basis_f.at[rows], basis_n.at[there], bf_send.at[f], bf_recv.at[o]).start()

    wait_bytes(l2maps.at[pl.ds(0, ngrp - 1)], map3_sem.at[1])

    def build3(t, carry):
        ids = lax.broadcasted_iota(jnp.int32, (ng3, nc2), 0)
        onehot3[:, block(t, nc2)] = jnp.where(ids == l2maps[t][0:1], F32(1.0), F32(0.0)).astype(BF16)
        return carry

    lax.fori_loop(0, ngrp, build3, 0)
    ld_l3inv.wait()
    own3 = onehot3[:, block(grp, nc2)].astype(F32).T.astype(BF16)
    l3rows = dot(own3, l3inv[...].astype(BF16)).astype(BF16)
    q3[...] = dot(l3rows, onehot3[...]).astype(BF16)

    wait_bytes(c_recv.at[pl.ds(0, nsub - 1)], c_sem.at[1])

    def build2(t, carry):
        recv2[:, block(t, nc1)] = c_recv[t, 0:kc, :]
        parts = c_recv[t, kc : 2 * kc, :].astype(F32)
        ids = lax.broadcasted_iota(jnp.int32, (ng2, nc1), 0)
        member = (parts[0:1] * 256.0 + parts[1:2]).astype(jnp.int32)
        onehot2[:, block(t + 1, nc1)] = jnp.where(ids == member, F32(1.0), F32(0.0)).astype(BF16)
        return carry

    lax.fori_loop(0, nsub, build2, 0)
    ld_l2inv.wait()
    res2 = dot_t(recv2[...], onehot2[:, nc1 : (nsub + 1) * nc1])
    local2 = fold_terms(dot_t(two_terms(res2), l2inv[...].astype(BF16)))

    wait_bytes(recv3.at[:, pl.ds(0, (ngrp - 1) * nc2)], z_sem.at[1])
    picked = two_terms(fold_terms(dot_t(two_terms(recv3[...]), q3[...])))
    sol2 = (local2 + fold_terms(dot(picked, l2basis_t))).astype(BF16)
    row = 2 * nx
    odd = lax.rem(sub, 2)

    def two(t):
        return pl.ds(pl.multiple_of((lax.rem(t, row) + lax.rem(t, 2)) * nc1, nc1), 2 * nc1)

    def spread(r, carry):
        far = ny - 1 - r
        y = lax.rem(at_y + far_first(far), ny)
        here = pl.ds(pl.multiple_of(y * row * nc1, nc1), (row + 2) * nc1)
        back[y] = dot(sol2, onehot2[:, here]).astype(BF16)

        def send_back(i, carry):
            j = row - 1 - i
            x = lax.rem(at_x + far_first(lax.div(j, 2)), nx)
            t = (y * nx + x) * 2 + lax.rem(at_c + lax.rem(j, 2), 2)

            @pl.when(t != sub)
            def _():
                pltpu.make_async_remote_copy(
                    src_ref=back.at[y, :, two(t)],
                    dst_ref=xtwo.at[block(sub, kc), :],
                    send_sem=back_sem.at[0],
                    recv_sem=back_sem.at[1],
                    device_id={"sub": t},
                    device_id_type=MESH,
                ).start()

            return carry

        return lax.fori_loop(0, row, send_back, carry)

    lax.fori_loop(0, ny, spread, 0)
    xtwo[block(sub, kc), :] = back[at_y, :, two(sub)]

    def send_across(i, carry):
        t = peer_sub(i)
        for f, step in ((2, -1), (3, 1)):

            @pl.when(exists[f])
            def _(f=f, step=step):
                pltpu.make_async_remote_copy(
                    src_ref=back.at[lax.div(t, row), :, block(lax.rem(t, row) + 1, nc1)],
                    dst_ref=xn.at[facing[f], block(sub, kc), :],
                    send_sem=xz_send.at[f - 2],
                    recv_sem=xz_recv.at[facing[f] - 2],
                    device_id={"sub": t, "grp": jnp.clip(grp + step, 0, ngrp - 1)},
                    device_id_type=MESH,
                ).start()

        return carry

    lax.fori_loop(0, nsub, send_across, 0)

    ld_schur.wait()
    wide_p = n_if // 2
    schur_p[:, 0:wide_p] = dot(schur[...], perm_t[:, 0:wide_p]).astype(BF16)

    wait_bytes(xtwo.at[pl.ds(0, (nsub - 1) * kc), :], back_sem.at[1])
    xcoef[...] = xtwo[:, block(1 - odd, nc1)]
    xn[odd] = xtwo[:, block(odd, nc1)]
    pltpu.make_async_remote_copy(
        src_ref=xcoef,
        dst_ref=xn.at[odd],
        send_sem=xf_send.at[0],
        recv_sem=xf_recv.at[0],
        device_id={"sub": sub + 1 - 2 * odd},
        device_id_type=MESH,
    ).start()

    schur_p[:, wide_p:] = dot(schur[...], perm_t[:, wide_p:]).astype(BF16)

    for f in range(4):

        @pl.when(exists[f])
        def _(f=f):
            wait_bytes(theirs_l.at[pl.ds(f * face, face)], lf_recv.at[f])
            wait_bytes(basis_n.at[pl.ds(f * face, face)], bf_recv.at[f])

        rows = slice(f * face, (f + 1) * face)
        base[rows, :] = mine_l[rows, :].astype(F32) + theirs_l[rows, :].astype(F32)
        pair[rows, 0:nc1] = (weights[f][:, 0:1] * basis_f[rows, :].astype(F32)).astype(BF16)
        pair[rows, nc1:] = (their_weights[f][:, 0:1] * basis_n[rows, :].astype(F32)).astype(BF16)

    def summed(f, here):
        rows = slice(f * face, (f + 1) * face)
        both = jnp.concatenate([xcoef[here, :], xn[f, here, :]], axis=1)
        return (base[rows, here] + dot_t(pair[rows, :], both)).astype(BF16)

    for f in (2, 3):

        @pl.when(exists[f])
        def _(f=f):
            wait_bytes(xn.at[f], xz_recv.at[f - 2])

    upper = jnp.concatenate([summed(2, slice(0, cols)), summed(3, slice(0, cols))], axis=0)
    sol_acc[...] = dot(perm_t[:, 2 * face :], upper).astype(BF16)
    img_acc[...] = dot(schur_p[:, 2 * face :], upper)

    wait_bytes(xn.at[1 - odd], xf_recv.at[0])
    stores = []
    for h in range(2):
        here = slice(h * half, (h + 1) * half)
        lower = jnp.concatenate([summed(0, here), summed(1, here)], axis=0)
        there = pl.ds(h * half, half)
        sol[:, here] = (sol_acc[:, here].astype(F32) + dot(perm_t[:, 0 : 2 * face], lower)).astype(BF16)
        stores.append(pltpu.make_async_copy(sol.at[:, there], sol_h.at[0, 0, :, there], out_sem.at[0, h]))
        stores[-1].start()
        img[:, here] = (img_acc[:, here] + dot(schur_p[:, 0 : 2 * face], lower)).astype(BF16)
        stores.append(pltpu.make_async_copy(img.at[:, there], img_h.at[0, 0, :, there], out_sem.at[1, h]))
        stores[-1].start()

    wait_bytes(t_src.at[pl.ds(0, nsub - 1)], t_sem.at[0])
    wait_bytes(c_src.at[pl.ds(0, nsub - 1)], c_sem.at[0])
    wait_bytes(l2maps.at[pl.ds(0, ngrp - 1)], map3_sem.at[0])
    wait_bytes(recv3.at[:, pl.ds(0, (ngrp - 1) * nc2)], z_sem.at[0])
    wait_bytes(xtwo.at[pl.ds(0, (nsub - 1) * kc), :], back_sem.at[0])
    wait_bytes(xcoef, xf_send.at[0])
    for f in range(4):

        @pl.when(exists[f])
        def _(f=f):
            rows = pl.ds(f * face, face)
            wait_bytes(mine_l.at[rows], lf_send.at[f])
            wait_bytes(basis_f.at[rows], bf_send.at[f])
            if f >= 2:
                wait_bytes(xn.at[f], xz_send.at[f - 2])

    for done in stores:
        done.wait()


def store(parts, sol, img, sol_h, img_h, sol_v, img_v, in_sem, out_sem):
    size = sol_v.shape[0] // parts
    moves = []
    for i in range(parts):
        rows = pl.ds(i * size, size)
        for j, (src, via, dst) in enumerate([(sol, sol_v, sol_h), (img, img_v, img_h)]):
            load = pltpu.make_async_copy(src.at[0, 0, rows], via.at[rows], in_sem.at[j, i])
            moves.append((load, pltpu.make_async_copy(via.at[rows], dst.at[0, 0, rows], out_sem.at[j, i])))
            load.start()
    for load, save in moves:
        load.wait()
        save.start()
    for load, save in moves:
        save.wait()


def shards(nsub, ngrp, *args):
    resid, order, stiff, schur, linv, basis, cmap, l2inv, l2basis, l2map, l3inv = args
    n_if, cols = resid.shape[2:]
    nc1 = basis.shape[3]
    ng2, nc2 = l2basis.shape[1:]
    ng3 = l3inv.shape[0]
    kc = cols // nsub
    nx, ny = plane(nsub)
    vmem = pltpu.VMEM
    dma = pltpu.SemaphoreType.DMA
    scratch = [
        vmem((n_if, cols), BF16),
        vmem((1, n_if), jnp.int32),
        vmem((n_if, nc1), BF16),
        vmem((1, nc1), jnp.int32),
        vmem((1, nc2), jnp.int32),
        pltpu.SMEM((ngrp, nsub), F32),
        vmem((n_if, n_if), BF16),
        vmem((n_if, n_if), BF16),
        vmem((ng2, ng2), F32),
        vmem((ng2, nc2), F32),
        vmem((ng3, ng3), F32),
        vmem((ngrp, 8, nc2), jnp.int32),
        vmem((n_if, n_if), BF16),
        vmem((n_if, n_if), BF16),
        vmem((n_if, LANES), F32),
        vmem((n_if, cols), BF16),
        vmem((nsub, kc, nc2), BF16),
        vmem((nsub, kc, nc2), BF16),
        vmem((nsub, 2 * kc, nc1), BF16),
        vmem((nsub, 2 * kc, nc1), BF16),
        vmem((kc, nsub * nc1), BF16),
        vmem((ng2, (nsub + 2) * nc1), BF16),
        vmem((ng3, ngrp * nc2), BF16),
        vmem((nc2, ngrp * nc2), BF16),
        vmem((kc, ngrp * nc2), F32),
        vmem((kc, nc2), F32),
        vmem((ny, kc, (2 * nx + 2) * nc1), BF16),
        vmem((cols, 2 * nc1), BF16),
        vmem((cols, nc1), BF16),
        vmem((4, cols, nc1), BF16),
        vmem((n_if, cols), BF16),
        vmem((n_if, cols), BF16),
        vmem((n_if, cols), BF16),
        vmem((n_if, nc1), BF16),
        vmem((n_if, nc1), BF16),
        vmem((n_if, n_if), BF16),
        vmem((n_if, cols), F32),
        vmem((n_if, 2 * nc1), BF16),
        vmem((n_if, cols), BF16),
        vmem((n_if, cols), F32),
        vmem((n_if, cols), BF16),
        vmem((n_if, cols), BF16),
        dma((11,)),
        dma((2, 2)),
        dma((2,)),
        dma((2,)),
        dma((2,)),
        dma((2,)),
        dma((2,)),
        dma((4,)),
        dma((4,)),
        dma((4,)),
        dma((4,)),
        dma((1,)),
        dma((1,)),
        dma((2,)),
        dma((2,)),
    ]
    flops = 2 * n_if * cols * n_if * 4 + 2 * n_if**3
    out = jax.ShapeDtypeStruct((1, 1, n_if, cols), BF16)
    any_ = pl.BlockSpec(memory_space=pl.ANY)
    done = pl.pallas_call(
        functools.partial(kernel, nsub, ngrp),
        out_shape=(out, out),
        in_specs=[any_] * 11,
        out_specs=(any_, any_),
        scratch_shapes=scratch,
        compiler_params=pltpu.CompilerParams(
            collective_id=0, has_side_effects=True, vmem_limit_bytes=60 * 1024 * 1024
        ),
        cost_estimate=pl.CostEstimate(flops=flops, bytes_accessed=11 << 20, transcendentals=0),
        name="bddc_apply",
    )(*args)
    return pl.pallas_call(
        functools.partial(store, 4),
        out_shape=(out, out),
        in_specs=[any_, any_],
        out_specs=(any_, any_),
        scratch_shapes=[vmem((n_if, cols), BF16), vmem((n_if, cols), BF16), dma((2, 4)), dma((2, 4))],
        compiler_params=pltpu.CompilerParams(vmem_limit_bytes=60 * 1024 * 1024),
        name="store",
    )(*done)


def solution(mesh):
    placed = (
        P("grp", "sub", None, None),
        P("grp", "sub", None),
        P(),
        P("grp", "sub", None, None),
        P("grp", "sub", None, None),
        P("grp", "sub", None, None),
        P("grp", "sub", None),
        P("grp", None, None),
        P("grp", None, None),
        P("grp", None),
        P(),
    )
    return jax.shard_map(
        functools.partial(shards, mesh.shape["sub"], mesh.shape["grp"]),
        mesh=mesh,
        in_specs=placed,
        out_specs=(P("grp", "sub", None, None), P("grp", "sub", None, None)),
        check_vma=False,
    )
```

```python
import functools

import jax
import jax.numpy as jnp
from jax import lax
from jax.experimental import pallas as pl
from jax.experimental.pallas import tpu as pltpu
from jax.sharding import PartitionSpec as P

MESH = pl.DeviceIdType.MESH
F32 = jnp.float32
BF16 = jnp.bfloat16
LANES = 128


def dot(a, b):
    return jnp.dot(a, b, preferred_element_type=F32)


def dot_t(a, b):
    return lax.dot_general(a, b, (((1,), (1,)), ((), ())), preferred_element_type=F32)


def two_terms(x):
    high = x.astype(BF16)
    low = (x - high.astype(F32)).astype(BF16)
    return jnp.concatenate([high, low], axis=0)


def fold_terms(x):
    half = x.shape[0] // 2
    return x[:half] + x[half:]


def block(index, size):
    return pl.ds(pl.multiple_of(index * size, size), size)


def plane(nsub):
    nx = 4 if nsub % 8 == 0 else 2
    return nx, nsub // (2 * nx)


def far_first(r):
    return r + lax.div(r, 2) - 2 * lax.div(r, 3)


def kernel(
    nsub,
    ngrp,
    resid_h,
    order_h,
    stiff_h,
    schur_h,
    linv_h,
    basis_h,
    cmap_h,
    l2inv_h,
    l2basis_h,
    l2map_h,
    l3inv_h,
    sol_h,
    img_h,
    resid,
    order_s,
    basis_s,
    cmap,
    l2map,
    stiff,
    schur,
    linv,
    l2inv,
    l2basis,
    l3inv,
    l2maps,
    perm_t,
    perm,
    dofw,
    weighted,
    t_src,
    t_recv,
    c_src,
    c_recv,
    recv2,
    onehot2,
    onehot3,
    q3,
    recv3,
    term3,
    back,
    xtwo,
    xcoef,
    xn,
    scaled,
    mine_l,
    theirs_l,
    basis_f,
    basis_n,
    schur_p,
    base,
    pair,
    sol_acc,
    img_acc,
    sol,
    img,
    in_sem,
    out_sem,
    map3_sem,
    t_sem,
    c_sem,
    z_sem,
    back_sem,
    lf_send,
    lf_recv,
    bf_send,
    bf_recv,
    xf_send,
    xf_recv,
    xz_send,
    xz_recv,
):
    grp = lax.axis_index("grp")
    sub = lax.axis_index("sub")
    n_if, cols = weighted.shape
    face = n_if // 4
    nc1 = xcoef.shape[1]
    ng2, nc2 = l2basis.shape
    ng3 = l3inv.shape[0]
    kc = cols // nsub
    half = cols // 2

    loads = [
        pltpu.make_async_copy(src, dst, in_sem.at[i])
        for i, (src, dst) in enumerate(
            [
                (order_h.at[0], order_s),
                (stiff_h, stiff),
                (cmap_h.at[0], cmap),
                (l2map_h, l2map),
                (basis_h.at[0, 0], basis_s),
                (l2basis_h.at[0], l2basis),
                (resid_h.at[0, 0], resid),
                (linv_h.at[0, 0], linv),
                (l2inv_h.at[0], l2inv),
                (l3inv_h, l3inv),
                (schur_h.at[0, 0], schur),
            ]
        )
    ]
    for load in loads[:8]:
        load.start()
    ld_order, ld_stiff, ld_cmap, ld_l2map, ld_basis, ld_l2basis, ld_resid, ld_linv, ld_l2inv, ld_l3inv, ld_schur = loads

    nx, ny = plane(nsub)
    at_y, at_x, at_c = lax.div(sub, 2 * nx), lax.rem(lax.div(sub, 2), nx), lax.rem(sub, 2)

    def peer_sub(i):
        j = nsub - 1 - i
        y = lax.rem(at_y + far_first(lax.div(j, 2 * nx)), ny)
        x = lax.rem(at_x + far_first(lax.rem(lax.div(j, 2), nx)), nx)
        return (y * nx + x) * 2 + lax.rem(at_c + lax.rem(j, 2), 2)

    def peer_grp(i):
        off = ngrp // 2 + lax.div(i + 1, 2) * (1 - 2 * lax.rem(i, 2))
        return lax.rem(grp + off, ngrp)

    barrier = pltpu.get_barrier_semaphore()

    def greet_sub(i, carry):
        pl.semaphore_signal(barrier, inc=1, device_id={"sub": peer_sub(i)}, device_id_type=MESH)
        return carry

    def greet_grp(i, carry):
        pl.semaphore_signal(barrier, inc=1, device_id={"grp": peer_grp(i)}, device_id_type=MESH)
        return carry

    lax.fori_loop(0, nsub - 1, greet_sub, 0)
    lax.fori_loop(0, ngrp - 1, greet_grp, 0)

    ld_stiff.wait()
    own = stiff[grp, sub]
    exists = [sub > 0, sub < nsub - 1, grp > 0, grp < ngrp - 1]
    weights, their_weights = [], []
    for f, (g, s) in enumerate(((grp, sub - 1), (grp, sub + 1), (grp - 1, sub), (grp + 1, sub))):
        other = stiff[jnp.clip(g, 0, ngrp - 1), jnp.clip(s, 0, nsub - 1)]
        here = jnp.full((8, face), exists[f].astype(jnp.int32), jnp.int32) > 0
        num, nbr = jnp.full((8, face), own, F32), jnp.full((8, face), other, F32)
        weights.append(jnp.where(here, num / (num + nbr), F32(1.0))[0:1])
        their_weights.append((nbr / (nbr + num))[0:1])
    all_weights = jnp.concatenate(weights, axis=1)

    onehot2[:, 0:nc1] = jnp.zeros((ng2, nc1), BF16)
    onehot2[:, (nsub + 1) * nc1 :] = jnp.zeros((ng2, nc1), BF16)
    for f in range(4):

        @pl.when(jnp.logical_not(exists[f]))
        def _(f=f):
            rows = slice(f * face, (f + 1) * face)
            theirs_l[rows, :] = jnp.zeros((face, cols), BF16)
            basis_n[rows, :] = jnp.zeros((face, nc1), BF16)
            xn[f] = jnp.zeros((cols, nc1), BF16)

    ld_cmap.wait()
    ld_l2map.wait()
    l2maps[grp] = jnp.broadcast_to(l2map[...], (8, nc2))
    ld_order.wait()
    order = order_s[...]

    def weigh(r, carry):
        rows = block(r, face)
        ids = lax.broadcasted_iota(jnp.int32, (face, n_if), 0) + r * face
        here = ids == order
        perm_t[rows, :] = jnp.where(here, F32(1.0), F32(0.0)).astype(BF16)
        dw = jnp.sum(jnp.where(here, all_weights, F32(0.0)), axis=1, keepdims=True)
        dofw[rows, :] = jnp.broadcast_to(dw, (face, LANES))
        return carry

    lax.fori_loop(0, 4, weigh, 0)
    ld_basis.wait()
    basis = basis_s[...]
    basis_t = basis.astype(F32).T.astype(BF16)
    ld_l2basis.wait()
    l2basis_t = l2basis[...].T.astype(BF16)
    own_ids = lax.broadcasted_iota(jnp.int32, (ng2, nc1), 0)
    own_map = jnp.where(own_ids == cmap[...], F32(1.0), F32(0.0)).astype(BF16)
    own_rows = dot(l2basis_t, own_map).astype(BF16)
    both_t = jnp.concatenate([basis_t, dot(own_rows, basis_t).astype(BF16)], axis=0)
    ld_resid.wait()
    for load in loads[8:]:
        load.start()
    wide = jnp.concatenate([dofw[...]] * (-(-cols // LANES)), axis=1)[:, :cols]
    weighted[...] = (wide * resid[...].astype(F32)).astype(BF16)
    coarse_t = dot(both_t, weighted[...]).T.astype(BF16)
    t_src[...] = coarse_t[:, nc1:].reshape(nsub, kc, nc2)
    c_src[:, 0:kc, :] = coarse_t[:, :nc1].reshape(nsub, kc, nc1)
    high = lax.shift_right_logical(cmap[...], 8)
    map_rows = jnp.concatenate(
        [high.astype(F32), (cmap[...] - high * 256).astype(F32), jnp.zeros((kc - 2, nc1), F32)], axis=0
    ).astype(BF16)
    c_src[:, kc : 2 * kc, :] = jnp.broadcast_to(map_rows[None], (nsub, kc, nc1))

    pl.semaphore_wait(barrier, nsub + ngrp - 2)

    def wait_bytes(ref, sem):
        pltpu.make_async_copy(ref, ref, sem).wait()

    def send_t(i, carry):
        t = peer_sub(i)
        pltpu.make_async_remote_copy(
            src_ref=t_src.at[t],
            dst_ref=t_recv.at[sub],
            send_sem=t_sem.at[0],
            recv_sem=t_sem.at[1],
            device_id={"sub": t},
            device_id_type=MESH,
        ).start()
        return carry

    def send_c(i, carry):
        t = peer_sub(i)
        pltpu.make_async_remote_copy(
            src_ref=c_src.at[t],
            dst_ref=c_recv.at[sub],
            send_sem=c_sem.at[0],
            recv_sem=c_sem.at[1],
            device_id={"sub": t},
            device_id_type=MESH,
        ).start()
        return carry

    def send_map3(i, carry):
        pltpu.make_async_remote_copy(
            src_ref=l2maps.at[grp],
            dst_ref=l2maps.at[grp],
            send_sem=map3_sem.at[0],
            recv_sem=map3_sem.at[1],
            device_id={"grp": peer_grp(i)},
            device_id_type=MESH,
        ).start()
        return carry

    lax.fori_loop(0, nsub - 1, send_t, 0)
    lax.fori_loop(0, ngrp - 1, send_map3, 0)
    lax.fori_loop(0, nsub - 1, send_c, 0)
    t_recv[sub] = t_src[sub]
    c_recv[sub] = c_src[sub]

    ld_linv.wait()
    scaled[...] = (wide * dot(linv[...], weighted[...])).astype(BF16)
    order_col = jnp.broadcast_to(order.astype(F32), (LANES, n_if)).T.astype(jnp.int32)

    def build_perm(b, carry):
        ids = lax.broadcasted_iota(jnp.int32, (n_if, LANES), 1) + b * LANES
        perm[:, block(b, LANES)] = jnp.where(ids == order_col, F32(1.0), F32(0.0)).astype(BF16)
        return carry

    lax.fori_loop(0, n_if // LANES, build_perm, 0)

    wait_bytes(t_recv.at[pl.ds(0, nsub - 1)], t_sem.at[1])
    term3[...] = jnp.sum(t_recv[...].astype(F32), axis=0)
    recv3[:, block(grp, nc2)] = term3[...]

    def send_z(i, carry):
        pltpu.make_async_remote_copy(
            src_ref=term3,
            dst_ref=recv3.at[:, block(grp, nc2)],
            send_sem=z_sem.at[0],
            recv_sem=z_sem.at[1],
            device_id={"grp": peer_grp(i)},
            device_id_type=MESH,
        ).start()
        return carry

    lax.fori_loop(0, ngrp - 1, send_z, 0)

    mine_l[...] = dot(perm[...], scaled[...]).astype(BF16)
    basis_f[...] = dot(perm[...], basis).astype(BF16)
    facing = (1, 0, 3, 2)

    def to_neighbour(f, src, dst, send_sem, recv_sem):
        axis, step = (("sub", -1), ("sub", 1), ("grp", -1), ("grp", 1))[f]
        size = nsub if axis == "sub" else ngrp
        return pltpu.make_async_remote_copy(
            src_ref=src,
            dst_ref=dst,
            send_sem=send_sem,
            recv_sem=recv_sem,
            device_id={axis: jnp.clip(lax.axis_index(axis) + step, 0, size - 1)},
            device_id_type=MESH,
        )

    for f in (2, 3, 0, 1):

        @pl.when(exists[f])
        def _(f=f):
            o = facing[f]
            rows, there = pl.ds(f * face, face), pl.ds(o * face, face)
            to_neighbour(f, mine_l.at[rows], theirs_l.at[there], lf_send.at[f], lf_recv.at[o]).start()
            to_neighbour(f, basis_f.at[rows], basis_n.at[there], bf_send.at[f], bf_recv.at[o]).start()

    wait_bytes(l2maps.at[pl.ds(0, ngrp - 1)], map3_sem.at[1])

    def build3(t, carry):
        ids = lax.broadcasted_iota(jnp.int32, (ng3, nc2), 0)
        onehot3[:, block(t, nc2)] = jnp.where(ids == l2maps[t][0:1], F32(1.0), F32(0.0)).astype(BF16)
        return carry

    lax.fori_loop(0, ngrp, build3, 0)
    ld_l3inv.wait()
    own3 = onehot3[:, block(grp, nc2)].astype(F32).T.astype(BF16)
    l3rows = dot(own3, l3inv[...].astype(BF16)).astype(BF16)
    q3[...] = dot(l3rows, onehot3[...]).astype(BF16)

    wait_bytes(c_recv.at[pl.ds(0, nsub - 1)], c_sem.at[1])

    def build2(t, carry):
        recv2[:, block(t, nc1)] = c_recv[t, 0:kc, :]
        parts = c_recv[t, kc : 2 * kc, :].astype(F32)
        ids = lax.broadcasted_iota(jnp.int32, (ng2, nc1), 0)
        member = (parts[0:1] * 256.0 + parts[1:2]).astype(jnp.int32)
        onehot2[:, block(t + 1, nc1)] = jnp.where(ids == member, F32(1.0), F32(0.0)).astype(BF16)
        return carry

    lax.fori_loop(0, nsub, build2, 0)
    ld_l2inv.wait()
    res2 = dot_t(recv2[...], onehot2[:, nc1 : (nsub + 1) * nc1])
    local2 = fold_terms(dot_t(two_terms(res2), l2inv[...].astype(BF16)))

    wait_bytes(recv3.at[:, pl.ds(0, (ngrp - 1) * nc2)], z_sem.at[1])
    picked = two_terms(fold_terms(dot_t(two_terms(recv3[...]), q3[...])))
    sol2 = (local2 + fold_terms(dot(picked, l2basis_t))).astype(BF16)
    row = 2 * nx
    odd = lax.rem(sub, 2)

    def two(t):
        return pl.ds(pl.multiple_of((lax.rem(t, row) + lax.rem(t, 2)) * nc1, nc1), 2 * nc1)

    def spread(r, carry):
        far = ny - 1 - r
        y = lax.rem(at_y + far_first(far), ny)
        here = pl.ds(pl.multiple_of(y * row * nc1, nc1), (row + 2) * nc1)
        back[y] = dot(sol2, onehot2[:, here]).astype(BF16)

        def send_back(i, carry):
            j = row - 1 - i
            x = lax.rem(at_x + far_first(lax.div(j, 2)), nx)
            t = (y * nx + x) * 2 + lax.rem(at_c + lax.rem(j, 2), 2)

            @pl.when(t != sub)
            def _():
                pltpu.make_async_remote_copy(
                    src_ref=back.at[y, :, two(t)],
                    dst_ref=xtwo.at[block(sub, kc), :],
                    send_sem=back_sem.at[0],
                    recv_sem=back_sem.at[1],
                    device_id={"sub": t},
                    device_id_type=MESH,
                ).start()

            return carry

        return lax.fori_loop(0, row, send_back, carry)

    lax.fori_loop(0, ny, spread, 0)
    xtwo[block(sub, kc), :] = back[at_y, :, two(sub)]

    def send_across(i, carry):
        t = peer_sub(i)
        for f, step in ((2, -1), (3, 1)):

            @pl.when(exists[f])
            def _(f=f, step=step):
                pltpu.make_async_remote_copy(
                    src_ref=back.at[lax.div(t, row), :, block(lax.rem(t, row) + 1, nc1)],
                    dst_ref=xn.at[facing[f], block(sub, kc), :],
                    send_sem=xz_send.at[f - 2],
                    recv_sem=xz_recv.at[facing[f] - 2],
                    device_id={"sub": t, "grp": jnp.clip(grp + step, 0, ngrp - 1)},
                    device_id_type=MESH,
                ).start()

        return carry

    lax.fori_loop(0, nsub, send_across, 0)

    ld_schur.wait()
    wide_p = n_if // 2
    schur_p[:, 0:wide_p] = dot(schur[...], perm_t[:, 0:wide_p]).astype(BF16)

    wait_bytes(xtwo.at[pl.ds(0, (nsub - 1) * kc), :], back_sem.at[1])
    xcoef[...] = xtwo[:, block(1 - odd, nc1)]
    xn[odd] = xtwo[:, block(odd, nc1)]
    pltpu.make_async_remote_copy(
        src_ref=xcoef,
        dst_ref=xn.at[odd],
        send_sem=xf_send.at[0],
        recv_sem=xf_recv.at[0],
        device_id={"sub": sub + 1 - 2 * odd},
        device_id_type=MESH,
    ).start()

    schur_p[:, wide_p:] = dot(schur[...], perm_t[:, wide_p:]).astype(BF16)

    for f in range(4):

        @pl.when(exists[f])
        def _(f=f):
            wait_bytes(theirs_l.at[pl.ds(f * face, face)], lf_recv.at[f])
            wait_bytes(basis_n.at[pl.ds(f * face, face)], bf_recv.at[f])

        rows = slice(f * face, (f + 1) * face)
        base[rows, :] = mine_l[rows, :].astype(F32) + theirs_l[rows, :].astype(F32)
        pair[rows, 0:nc1] = (weights[f][:, 0:1] * basis_f[rows, :].astype(F32)).astype(BF16)
        pair[rows, nc1:] = (their_weights[f][:, 0:1] * basis_n[rows, :].astype(F32)).astype(BF16)

    def summed(f, here):
        rows = slice(f * face, (f + 1) * face)
        both = jnp.concatenate([xcoef[here, :], xn[f, here, :]], axis=1)
        return (base[rows, here] + dot_t(pair[rows, :], both)).astype(BF16)

    wait_bytes(xn.at[1 - odd], xf_recv.at[0])
    lower = jnp.concatenate([summed(0, slice(0, cols)), summed(1, slice(0, cols))], axis=0)
    sol_acc[...] = dot(perm_t[:, 0 : 2 * face], lower).astype(BF16)
    img_acc[...] = dot(schur_p[:, 0 : 2 * face], lower)

    for f in (2, 3):

        @pl.when(exists[f])
        def _(f=f):
            wait_bytes(xn.at[f], xz_recv.at[f - 2])

    stores = []
    for h in range(2):
        here = slice(h * half, (h + 1) * half)
        upper = jnp.concatenate([summed(2, here), summed(3, here)], axis=0)
        there = pl.ds(h * half, half)
        sol[:, here] = (sol_acc[:, here].astype(F32) + dot(perm_t[:, 2 * face :], upper)).astype(BF16)
        stores.append(pltpu.make_async_copy(sol.at[:, there], sol_h.at[0, 0, :, there], out_sem.at[0, h]))
        stores[-1].start()
        img[:, here] = (img_acc[:, here] + dot(schur_p[:, 2 * face :], upper)).astype(BF16)
        stores.append(pltpu.make_async_copy(img.at[:, there], img_h.at[0, 0, :, there], out_sem.at[1, h]))
        stores[-1].start()

    wait_bytes(t_src.at[pl.ds(0, nsub - 1)], t_sem.at[0])
    wait_bytes(c_src.at[pl.ds(0, nsub - 1)], c_sem.at[0])
    wait_bytes(l2maps.at[pl.ds(0, ngrp - 1)], map3_sem.at[0])
    wait_bytes(recv3.at[:, pl.ds(0, (ngrp - 1) * nc2)], z_sem.at[0])
    wait_bytes(xtwo.at[pl.ds(0, (nsub - 1) * kc), :], back_sem.at[0])
    wait_bytes(xcoef, xf_send.at[0])
    for f in range(4):

        @pl.when(exists[f])
        def _(f=f):
            rows = pl.ds(f * face, face)
            wait_bytes(mine_l.at[rows], lf_send.at[f])
            wait_bytes(basis_f.at[rows], bf_send.at[f])
            if f >= 2:
                wait_bytes(xn.at[f], xz_send.at[f - 2])

    for done in stores:
        done.wait()


def store(parts, sol, img, sol_h, img_h, sol_v, img_v, in_sem, out_sem):
    size = sol_v.shape[0] // parts
    moves = []
    for i in range(parts):
        rows = pl.ds(i * size, size)
        for j, (src, via, dst) in enumerate([(sol, sol_v, sol_h), (img, img_v, img_h)]):
            load = pltpu.make_async_copy(src.at[0, 0, rows], via.at[rows], in_sem.at[j, i])
            moves.append((load, pltpu.make_async_copy(via.at[rows], dst.at[0, 0, rows], out_sem.at[j, i])))
            load.start()
    for load, save in moves:
        load.wait()
        save.start()
    for load, save in moves:
        save.wait()


def shards(nsub, ngrp, *args):
    resid, order, stiff, schur, linv, basis, cmap, l2inv, l2basis, l2map, l3inv = args
    n_if, cols = resid.shape[2:]
    nc1 = basis.shape[3]
    ng2, nc2 = l2basis.shape[1:]
    ng3 = l3inv.shape[0]
    kc = cols // nsub
    nx, ny = plane(nsub)
    vmem = pltpu.VMEM
    dma = pltpu.SemaphoreType.DMA
    scratch = [
        vmem((n_if, cols), BF16),
        vmem((1, n_if), jnp.int32),
        vmem((n_if, nc1), BF16),
        vmem((1, nc1), jnp.int32),
        vmem((1, nc2), jnp.int32),
        pltpu.SMEM((ngrp, nsub), F32),
        vmem((n_if, n_if), BF16),
        vmem((n_if, n_if), BF16),
        vmem((ng2, ng2), F32),
        vmem((ng2, nc2), F32),
        vmem((ng3, ng3), F32),
        vmem((ngrp, 8, nc2), jnp.int32),
        vmem((n_if, n_if), BF16),
        vmem((n_if, n_if), BF16),
        vmem((n_if, LANES), F32),
        vmem((n_if, cols), BF16),
        vmem((nsub, kc, nc2), BF16),
        vmem((nsub, kc, nc2), BF16),
        vmem((nsub, 2 * kc, nc1), BF16),
        vmem((nsub, 2 * kc, nc1), BF16),
        vmem((kc, nsub * nc1), BF16),
        vmem((ng2, (nsub + 2) * nc1), BF16),
        vmem((ng3, ngrp * nc2), BF16),
        vmem((nc2, ngrp * nc2), BF16),
        vmem((kc, ngrp * nc2), F32),
        vmem((kc, nc2), F32),
        vmem((ny, kc, (2 * nx + 2) * nc1), BF16),
        vmem((cols, 2 * nc1), BF16),
        vmem((cols, nc1), BF16),
        vmem((4, cols, nc1), BF16),
        vmem((n_if, cols), BF16),
        vmem((n_if, cols), BF16),
        vmem((n_if, cols), BF16),
        vmem((n_if, nc1), BF16),
        vmem((n_if, nc1), BF16),
        vmem((n_if, n_if), BF16),
        vmem((n_if, cols), F32),
        vmem((n_if, 2 * nc1), BF16),
        vmem((n_if, cols), BF16),
        vmem((n_if, cols), F32),
        vmem((n_if, cols), BF16),
        vmem((n_if, cols), BF16),
        dma((11,)),
        dma((2, 2)),
        dma((2,)),
        dma((2,)),
        dma((2,)),
        dma((2,)),
        dma((2,)),
        dma((4,)),
        dma((4,)),
        dma((4,)),
        dma((4,)),
        dma((1,)),
        dma((1,)),
        dma((2,)),
        dma((2,)),
    ]
    flops = 2 * n_if * cols * n_if * 4 + 2 * n_if**3
    out = jax.ShapeDtypeStruct((1, 1, n_if, cols), BF16)
    any_ = pl.BlockSpec(memory_space=pl.ANY)
    done = pl.pallas_call(
        functools.partial(kernel, nsub, ngrp),
        out_shape=(out, out),
        in_specs=[any_] * 11,
        out_specs=(any_, any_),
        scratch_shapes=scratch,
        compiler_params=pltpu.CompilerParams(
            collective_id=0, has_side_effects=True, vmem_limit_bytes=60 * 1024 * 1024
        ),
        cost_estimate=pl.CostEstimate(flops=flops, bytes_accessed=11 << 20, transcendentals=0),
        name="bddc_apply",
    )(*args)
    return pl.pallas_call(
        functools.partial(store, 4),
        out_shape=(out, out),
        in_specs=[any_, any_],
        out_specs=(any_, any_),
        scratch_shapes=[vmem((n_if, cols), BF16), vmem((n_if, cols), BF16), dma((2, 4)), dma((2, 4))],
        compiler_params=pltpu.CompilerParams(vmem_limit_bytes=60 * 1024 * 1024),
        name="store",
    )(*done)


def solution(mesh):
    placed = (
        P("grp", "sub", None, None),
        P("grp", "sub", None),
        P(),
        P("grp", "sub", None, None),
        P("grp", "sub", None, None),
        P("grp", "sub", None, None),
        P("grp", "sub", None),
        P("grp", None, None),
        P("grp", None, None),
        P("grp", None),
        P(),
    )
    return jax.shard_map(
        functools.partial(shards, mesh.shape["sub"], mesh.shape["grp"]),
        mesh=mesh,
        in_specs=placed,
        out_specs=(P("grp", "sub", None, None), P("grp", "sub", None, None)),
        check_vma=False,
    )
```

```python
import functools

import jax
import jax.numpy as jnp
from jax import lax
from jax.experimental import pallas as pl
from jax.experimental.pallas import tpu as pltpu
from jax.sharding import PartitionSpec as P

MESH = pl.DeviceIdType.MESH
F32 = jnp.float32
BF16 = jnp.bfloat16
LANES = 128


def dot(a, b):
    return jnp.dot(a, b, preferred_element_type=F32)


def dot_t(a, b):
    return lax.dot_general(a, b, (((1,), (1,)), ((), ())), preferred_element_type=F32)


def two_terms(x):
    high = x.astype(BF16)
    low = (x - high.astype(F32)).astype(BF16)
    return jnp.concatenate([high, low], axis=0)


def fold_terms(x):
    half = x.shape[0] // 2
    return x[:half] + x[half:]


def block(index, size):
    return pl.ds(pl.multiple_of(index * size, size), size)


def plane(nsub):
    nx = 4 if nsub % 8 == 0 else 2
    return nx, nsub // (2 * nx)


def far_first(r):
    return r + lax.div(r, 2) - 2 * lax.div(r, 3)


def kernel(
    nsub,
    ngrp,
    resid_h,
    order_h,
    stiff_h,
    schur_h,
    linv_h,
    basis_h,
    cmap_h,
    l2inv_h,
    l2basis_h,
    l2map_h,
    l3inv_h,
    sol_h,
    img_h,
    resid,
    order_s,
    basis_s,
    cmap,
    l2map,
    stiff,
    schur,
    linv,
    l2inv,
    l2basis,
    l3inv,
    l2maps,
    perm_t,
    perm,
    dofw,
    weighted,
    t_src,
    t_recv,
    c_src,
    c_recv,
    recv2,
    onehot2,
    onehot3,
    q3,
    recv3,
    term3,
    back,
    xtwo,
    xcoef,
    xn,
    scaled,
    mine_l,
    theirs_l,
    basis_f,
    basis_n,
    schur_p,
    base,
    pair,
    sol_acc,
    img_acc,
    sol,
    img,
    in_sem,
    out_sem,
    map3_sem,
    t_sem,
    c_sem,
    z_sem,
    back_sem,
    lf_send,
    lf_recv,
    bf_send,
    bf_recv,
    xf_send,
    xf_recv,
    xz_send,
    xz_recv,
):
    grp = lax.axis_index("grp")
    sub = lax.axis_index("sub")
    n_if, cols = weighted.shape
    face = n_if // 4
    nc1 = xcoef.shape[1]
    ng2, nc2 = l2basis.shape
    ng3 = l3inv.shape[0]
    kc = cols // nsub
    half = cols // 2

    loads = [
        pltpu.make_async_copy(src, dst, in_sem.at[i])
        for i, (src, dst) in enumerate(
            [
                (order_h.at[0], order_s),
                (stiff_h, stiff),
                (cmap_h.at[0], cmap),
                (l2map_h, l2map),
                (basis_h.at[0, 0], basis_s),
                (l2basis_h.at[0], l2basis),
                (resid_h.at[0, 0], resid),
                (linv_h.at[0, 0], linv),
                (l2inv_h.at[0], l2inv),
                (l3inv_h, l3inv),
                (schur_h.at[0, 0], schur),
            ]
        )
    ]
    for load in loads[:8]:
        load.start()
    ld_order, ld_stiff, ld_cmap, ld_l2map, ld_basis, ld_l2basis, ld_resid, ld_linv, ld_l2inv, ld_l3inv, ld_schur = loads

    nx, ny = plane(nsub)
    at_y, at_x, at_c = lax.div(sub, 2 * nx), lax.rem(lax.div(sub, 2), nx), lax.rem(sub, 2)

    row = 2 * nx
    far_x = [lax.rem(at_x + d, nx) * 2 for d in ((2, 3, 1, 0) if nx == 4 else (1, 0))]
    far_c = [lax.rem(at_c + d, 2) for d in (1, 0)]

    def row_at(r):
        return lax.rem(at_y + far_first(ny - 1 - r), ny)

    def over_row(y, visit, with_self=False):
        for i, x in enumerate(far_x):
            for j, c in enumerate(far_c):
                t = y * row + x + c
                if with_self or (i, j) != (nx - 1, 1):
                    visit(t)
                else:
                    pl.when(t != sub)(functools.partial(visit, t))

    def over_plane(visit):
        def body(r, carry):
            over_row(row_at(r), visit)
            return carry

        lax.fori_loop(0, ny, body, 0)

    def peer_grp(i):
        off = ngrp // 2 + lax.div(i + 1, 2) * (1 - 2 * lax.rem(i, 2))
        return lax.rem(grp + off, ngrp)

    barrier = pltpu.get_barrier_semaphore()

    def greet_sub(t):
        pl.semaphore_signal(barrier, inc=1, device_id={"sub": t}, device_id_type=MESH)

    def greet_grp(i, carry):
        pl.semaphore_signal(barrier, inc=1, device_id={"grp": peer_grp(i)}, device_id_type=MESH)
        return carry

    over_plane(greet_sub)
    lax.fori_loop(0, ngrp - 1, greet_grp, 0)

    ld_stiff.wait()
    own = stiff[grp, sub]
    exists = [sub > 0, sub < nsub - 1, grp > 0, grp < ngrp - 1]
    weights, their_weights = [], []
    for f, (g, s) in enumerate(((grp, sub - 1), (grp, sub + 1), (grp - 1, sub), (grp + 1, sub))):
        other = stiff[jnp.clip(g, 0, ngrp - 1), jnp.clip(s, 0, nsub - 1)]
        here = jnp.full((8, face), exists[f].astype(jnp.int32), jnp.int32) > 0
        num, nbr = jnp.full((8, face), own, F32), jnp.full((8, face), other, F32)
        weights.append(jnp.where(here, num / (num + nbr), F32(1.0))[0:1])
        their_weights.append((nbr / (nbr + num))[0:1])
    all_weights = jnp.concatenate(weights, axis=1)

    onehot2[:, 0:nc1] = jnp.zeros((ng2, nc1), BF16)
    onehot2[:, (nsub + 1) * nc1 :] = jnp.zeros((ng2, nc1), BF16)
    for f in range(4):

        @pl.when(jnp.logical_not(exists[f]))
        def _(f=f):
            rows = slice(f * face, (f + 1) * face)
            theirs_l[rows, :] = jnp.zeros((face, cols), BF16)
            basis_n[rows, :] = jnp.zeros((face, nc1), BF16)
            xn[f] = jnp.zeros((cols, nc1), BF16)

    ld_cmap.wait()
    ld_l2map.wait()
    l2maps[grp] = jnp.broadcast_to(l2map[...], (8, nc2))
    ld_order.wait()
    order = order_s[...]

    def weigh(r, carry):
        rows = block(r, face)
        ids = lax.broadcasted_iota(jnp.int32, (face, n_if), 0) + r * face
        here = ids == order
        perm_t[rows, :] = jnp.where(here, F32(1.0), F32(0.0)).astype(BF16)
        dw = jnp.sum(jnp.where(here, all_weights, F32(0.0)), axis=1, keepdims=True)
        dofw[rows, :] = jnp.broadcast_to(dw, (face, LANES))
        return carry

    lax.fori_loop(0, 4, weigh, 0)
    ld_basis.wait()
    basis = basis_s[...]
    basis_t = basis.astype(F32).T.astype(BF16)
    ld_l2basis.wait()
    l2basis_t = l2basis[...].T.astype(BF16)
    own_ids = lax.broadcasted_iota(jnp.int32, (ng2, nc1), 0)
    own_map = jnp.where(own_ids == cmap[...], F32(1.0), F32(0.0)).astype(BF16)
    own_rows = dot(l2basis_t, own_map).astype(BF16)
    both_t = jnp.concatenate([basis_t, dot(own_rows, basis_t).astype(BF16)], axis=0)
    ld_resid.wait()
    for load in loads[8:]:
        load.start()
    wide = jnp.concatenate([dofw[...]] * (-(-cols // LANES)), axis=1)[:, :cols]
    weighted[...] = (wide * resid[...].astype(F32)).astype(BF16)
    coarse_t = dot(both_t, weighted[...]).T.astype(BF16)
    t_src[...] = coarse_t[:, nc1:].reshape(nsub, kc, nc2)
    c_src[:, 0:kc, :] = coarse_t[:, :nc1].reshape(nsub, kc, nc1)
    high = lax.shift_right_logical(cmap[...], 8)
    map_rows = jnp.concatenate(
        [high.astype(F32), (cmap[...] - high * 256).astype(F32), jnp.zeros((kc - 2, nc1), F32)], axis=0
    ).astype(BF16)
    c_src[:, kc : 2 * kc, :] = jnp.broadcast_to(map_rows[None], (nsub, kc, nc1))

    pl.semaphore_wait(barrier, nsub + ngrp - 2)

    def wait_bytes(ref, sem):
        pltpu.make_async_copy(ref, ref, sem).wait()

    def send_t(t):
        pltpu.make_async_remote_copy(
            src_ref=t_src.at[t],
            dst_ref=t_recv.at[sub],
            send_sem=t_sem.at[0],
            recv_sem=t_sem.at[1],
            device_id={"sub": t},
            device_id_type=MESH,
        ).start()

    def send_c(t):
        pltpu.make_async_remote_copy(
            src_ref=c_src.at[t],
            dst_ref=c_recv.at[sub],
            send_sem=c_sem.at[0],
            recv_sem=c_sem.at[1],
            device_id={"sub": t},
            device_id_type=MESH,
        ).start()

    def send_map3(i, carry):
        pltpu.make_async_remote_copy(
            src_ref=l2maps.at[grp],
            dst_ref=l2maps.at[grp],
            send_sem=map3_sem.at[0],
            recv_sem=map3_sem.at[1],
            device_id={"grp": peer_grp(i)},
            device_id_type=MESH,
        ).start()
        return carry

    over_plane(send_t)
    lax.fori_loop(0, ngrp - 1, send_map3, 0)
    over_plane(send_c)
    t_recv[sub] = t_src[sub]
    c_recv[sub] = c_src[sub]

    ld_linv.wait()
    scaled[...] = (wide * dot(linv[...], weighted[...])).astype(BF16)
    order_col = jnp.broadcast_to(order.astype(F32), (LANES, n_if)).T.astype(jnp.int32)

    def build_perm(b, carry):
        ids = lax.broadcasted_iota(jnp.int32, (n_if, LANES), 1) + b * LANES
        perm[:, block(b, LANES)] = jnp.where(ids == order_col, F32(1.0), F32(0.0)).astype(BF16)
        return carry

    lax.fori_loop(0, n_if // LANES, build_perm, 0)

    wait_bytes(t_recv.at[pl.ds(0, nsub - 1)], t_sem.at[1])
    term3[...] = jnp.sum(t_recv[...].astype(F32), axis=0)
    recv3[:, block(grp, nc2)] = term3[...]

    def send_z(i, carry):
        pltpu.make_async_remote_copy(
            src_ref=term3,
            dst_ref=recv3.at[:, block(grp, nc2)],
            send_sem=z_sem.at[0],
            recv_sem=z_sem.at[1],
            device_id={"grp": peer_grp(i)},
            device_id_type=MESH,
        ).start()
        return carry

    lax.fori_loop(0, ngrp - 1, send_z, 0)

    mine_l[...] = dot(perm[...], scaled[...]).astype(BF16)
    basis_f[...] = dot(perm[...], basis).astype(BF16)
    facing = (1, 0, 3, 2)

    def to_neighbour(f, src, dst, send_sem, recv_sem):
        axis, step = (("sub", -1), ("sub", 1), ("grp", -1), ("grp", 1))[f]
        size = nsub if axis == "sub" else ngrp
        return pltpu.make_async_remote_copy(
            src_ref=src,
            dst_ref=dst,
            send_sem=send_sem,
            recv_sem=recv_sem,
            device_id={axis: jnp.clip(lax.axis_index(axis) + step, 0, size - 1)},
            device_id_type=MESH,
        )

    for f in (2, 3, 0, 1):

        @pl.when(exists[f])
        def _(f=f):
            o = facing[f]
            rows, there = pl.ds(f * face, face), pl.ds(o * face, face)
            to_neighbour(f, mine_l.at[rows], theirs_l.at[there], lf_send.at[f], lf_recv.at[o]).start()
            to_neighbour(f, basis_f.at[rows], basis_n.at[there], bf_send.at[f], bf_recv.at[o]).start()

    wait_bytes(l2maps.at[pl.ds(0, ngrp - 1)], map3_sem.at[1])

    def build3(t, carry):
        ids = lax.broadcasted_iota(jnp.int32, (ng3, nc2), 0)
        onehot3[:, block(t, nc2)] = jnp.where(ids == l2maps[t][0:1], F32(1.0), F32(0.0)).astype(BF16)
        return carry

    lax.fori_loop(0, ngrp, build3, 0)
    ld_l3inv.wait()
    own3 = onehot3[:, block(grp, nc2)].astype(F32).T.astype(BF16)
    l3rows = dot(own3, l3inv[...].astype(BF16)).astype(BF16)
    q3[...] = dot(l3rows, onehot3[...]).astype(BF16)

    wait_bytes(c_recv.at[pl.ds(0, nsub - 1)], c_sem.at[1])

    def build2(t, carry):
        recv2[:, block(t, nc1)] = c_recv[t, 0:kc, :]
        parts = c_recv[t, kc : 2 * kc, :].astype(F32)
        ids = lax.broadcasted_iota(jnp.int32, (ng2, nc1), 0)
        member = (parts[0:1] * 256.0 + parts[1:2]).astype(jnp.int32)
        onehot2[:, block(t + 1, nc1)] = jnp.where(ids == member, F32(1.0), F32(0.0)).astype(BF16)
        return carry

    lax.fori_loop(0, nsub, build2, 0)
    ld_l2inv.wait()
    res2 = dot_t(recv2[...], onehot2[:, nc1 : (nsub + 1) * nc1])
    local2 = fold_terms(dot_t(two_terms(res2), l2inv[...].astype(BF16)))

    wait_bytes(recv3.at[:, pl.ds(0, (ngrp - 1) * nc2)], z_sem.at[1])
    picked = two_terms(fold_terms(dot_t(two_terms(recv3[...]), q3[...])))
    sol2 = (local2 + fold_terms(dot(picked, l2basis_t))).astype(BF16)
    odd = lax.rem(sub, 2)

    def two(t):
        return pl.ds(pl.multiple_of((lax.rem(t, row) + lax.rem(t, 2)) * nc1, nc1), 2 * nc1)

    def spread(r, carry):
        y = row_at(r)
        here = pl.ds(pl.multiple_of(y * row * nc1, nc1), (row + 2) * nc1)
        back[y] = dot(sol2, onehot2[:, here]).astype(BF16)

        def send_back(t):
            pltpu.make_async_remote_copy(
                src_ref=back.at[y, :, two(t)],
                dst_ref=xtwo.at[block(sub, kc), :],
                send_sem=back_sem.at[0],
                recv_sem=back_sem.at[1],
                device_id={"sub": t},
                device_id_type=MESH,
            ).start()

        over_row(y, send_back)
        return carry

    lax.fori_loop(0, ny, spread, 0)
    xtwo[block(sub, kc), :] = back[at_y, :, two(sub)]

    def send_across(r, carry):
        y = row_at(r)
        for f, step in ((2, -1), (3, 1)):

            def send(t, f=f, step=step):
                pltpu.make_async_remote_copy(
                    src_ref=back.at[y, :, block(t - y * row + 1, nc1)],
                    dst_ref=xn.at[facing[f], block(sub, kc), :],
                    send_sem=xz_send.at[f - 2],
                    recv_sem=xz_recv.at[facing[f] - 2],
                    device_id={"sub": t, "grp": jnp.clip(grp + step, 0, ngrp - 1)},
                    device_id_type=MESH,
                ).start()

            pl.when(exists[f])(functools.partial(over_row, y, send, True))

        return carry

    lax.fori_loop(0, ny, send_across, 0)

    ld_schur.wait()
    wide_p = n_if // 2
    schur_p[:, 0:wide_p] = dot(schur[...], perm_t[:, 0:wide_p]).astype(BF16)

    wait_bytes(xtwo.at[pl.ds(0, (nsub - 1) * kc), :], back_sem.at[1])
    xcoef[...] = xtwo[:, block(1 - odd, nc1)]
    xn[odd] = xtwo[:, block(odd, nc1)]
    pltpu.make_async_remote_copy(
        src_ref=xcoef,
        dst_ref=xn.at[odd],
        send_sem=xf_send.at[0],
        recv_sem=xf_recv.at[0],
        device_id={"sub": sub + 1 - 2 * odd},
        device_id_type=MESH,
    ).start()

    schur_p[:, wide_p:] = dot(schur[...], perm_t[:, wide_p:]).astype(BF16)

    for f in range(4):

        @pl.when(exists[f])
        def _(f=f):
            wait_bytes(theirs_l.at[pl.ds(f * face, face)], lf_recv.at[f])
            wait_bytes(basis_n.at[pl.ds(f * face, face)], bf_recv.at[f])

        rows = slice(f * face, (f + 1) * face)
        base[rows, :] = mine_l[rows, :].astype(F32) + theirs_l[rows, :].astype(F32)
        pair[rows, 0:nc1] = (weights[f][:, 0:1] * basis_f[rows, :].astype(F32)).astype(BF16)
        pair[rows, nc1:] = (their_weights[f][:, 0:1] * basis_n[rows, :].astype(F32)).astype(BF16)

    def summed(f, here):
        rows = slice(f * face, (f + 1) * face)
        both = jnp.concatenate([xcoef[here, :], xn[f, here, :]], axis=1)
        return (base[rows, here] + dot_t(pair[rows, :], both)).astype(BF16)

    wait_bytes(xn.at[1 - odd], xf_recv.at[0])
    lower = jnp.concatenate([summed(0, slice(0, cols)), summed(1, slice(0, cols))], axis=0)
    sol_acc[...] = dot(perm_t[:, 0 : 2 * face], lower).astype(BF16)
    img_acc[...] = dot(schur_p[:, 0 : 2 * face], lower)

    for f in (2, 3):

        @pl.when(exists[f])
        def _(f=f):
            wait_bytes(xn.at[f], xz_recv.at[f - 2])

    stores = []
    for h in range(2):
        here = slice(h * half, (h + 1) * half)
        upper = jnp.concatenate([summed(2, here), summed(3, here)], axis=0)
        there = pl.ds(h * half, half)
        sol[:, here] = (sol_acc[:, here].astype(F32) + dot(perm_t[:, 2 * face :], upper)).astype(BF16)
        stores.append(pltpu.make_async_copy(sol.at[:, there], sol_h.at[0, 0, :, there], out_sem.at[0, h]))
        stores[-1].start()
        img[:, here] = (img_acc[:, here] + dot(schur_p[:, 2 * face :], upper)).astype(BF16)
        stores.append(pltpu.make_async_copy(img.at[:, there], img_h.at[0, 0, :, there], out_sem.at[1, h]))
        stores[-1].start()

    wait_bytes(t_src.at[pl.ds(0, nsub - 1)], t_sem.at[0])
    wait_bytes(c_src.at[pl.ds(0, nsub - 1)], c_sem.at[0])
    wait_bytes(l2maps.at[pl.ds(0, ngrp - 1)], map3_sem.at[0])
    wait_bytes(recv3.at[:, pl.ds(0, (ngrp - 1) * nc2)], z_sem.at[0])
    wait_bytes(xtwo.at[pl.ds(0, (nsub - 1) * kc), :], back_sem.at[0])
    wait_bytes(xcoef, xf_send.at[0])
    for f in range(4):

        @pl.when(exists[f])
        def _(f=f):
            rows = pl.ds(f * face, face)
            wait_bytes(mine_l.at[rows], lf_send.at[f])
            wait_bytes(basis_f.at[rows], bf_send.at[f])
            if f >= 2:
                wait_bytes(xn.at[f], xz_send.at[f - 2])

    for done in stores:
        done.wait()


def store(parts, sol, img, sol_h, img_h, sol_v, img_v, in_sem, out_sem):
    size = sol_v.shape[0] // parts
    moves = []
    for i in range(parts):
        rows = pl.ds(i * size, size)
        for j, (src, via, dst) in enumerate([(sol, sol_v, sol_h), (img, img_v, img_h)]):
            load = pltpu.make_async_copy(src.at[0, 0, rows], via.at[rows], in_sem.at[j, i])
            moves.append((load, pltpu.make_async_copy(via.at[rows], dst.at[0, 0, rows], out_sem.at[j, i])))
            load.start()
    for load, save in moves:
        load.wait()
        save.start()
    for load, save in moves:
        save.wait()


def shards(nsub, ngrp, *args):
    resid, order, stiff, schur, linv, basis, cmap, l2inv, l2basis, l2map, l3inv = args
    n_if, cols = resid.shape[2:]
    nc1 = basis.shape[3]
    ng2, nc2 = l2basis.shape[1:]
    ng3 = l3inv.shape[0]
    kc = cols // nsub
    nx, ny = plane(nsub)
    vmem = pltpu.VMEM
    dma = pltpu.SemaphoreType.DMA
    scratch = [
        vmem((n_if, cols), BF16),
        vmem((1, n_if), jnp.int32),
        vmem((n_if, nc1), BF16),
        vmem((1, nc1), jnp.int32),
        vmem((1, nc2), jnp.int32),
        pltpu.SMEM((ngrp, nsub), F32),
        vmem((n_if, n_if), BF16),
        vmem((n_if, n_if), BF16),
        vmem((ng2, ng2), F32),
        vmem((ng2, nc2), F32),
        vmem((ng3, ng3), F32),
        vmem((ngrp, 8, nc2), jnp.int32),
        vmem((n_if, n_if), BF16),
        vmem((n_if, n_if), BF16),
        vmem((n_if, LANES), F32),
        vmem((n_if, cols), BF16),
        vmem((nsub, kc, nc2), BF16),
        vmem((nsub, kc, nc2), BF16),
        vmem((nsub, 2 * kc, nc1), BF16),
        vmem((nsub, 2 * kc, nc1), BF16),
        vmem((kc, nsub * nc1), BF16),
        vmem((ng2, (nsub + 2) * nc1), BF16),
        vmem((ng3, ngrp * nc2), BF16),
        vmem((nc2, ngrp * nc2), BF16),
        vmem((kc, ngrp * nc2), F32),
        vmem((kc, nc2), F32),
        vmem((ny, kc, (2 * nx + 2) * nc1), BF16),
        vmem((cols, 2 * nc1), BF16),
        vmem((cols, nc1), BF16),
        vmem((4, cols, nc1), BF16),
        vmem((n_if, cols), BF16),
        vmem((n_if, cols), BF16),
        vmem((n_if, cols), BF16),
        vmem((n_if, nc1), BF16),
        vmem((n_if, nc1), BF16),
        vmem((n_if, n_if), BF16),
        vmem((n_if, cols), F32),
        vmem((n_if, 2 * nc1), BF16),
        vmem((n_if, cols), BF16),
        vmem((n_if, cols), F32),
        vmem((n_if, cols), BF16),
        vmem((n_if, cols), BF16),
        dma((11,)),
        dma((2, 2)),
        dma((2,)),
        dma((2,)),
        dma((2,)),
        dma((2,)),
        dma((2,)),
        dma((4,)),
        dma((4,)),
        dma((4,)),
        dma((4,)),
        dma((1,)),
        dma((1,)),
        dma((2,)),
        dma((2,)),
    ]
    flops = 2 * n_if * cols * n_if * 4 + 2 * n_if**3
    out = jax.ShapeDtypeStruct((1, 1, n_if, cols), BF16)
    any_ = pl.BlockSpec(memory_space=pl.ANY)
    done = pl.pallas_call(
        functools.partial(kernel, nsub, ngrp),
        out_shape=(out, out),
        in_specs=[any_] * 11,
        out_specs=(any_, any_),
        scratch_shapes=scratch,
        compiler_params=pltpu.CompilerParams(
            collective_id=0, has_side_effects=True, vmem_limit_bytes=60 * 1024 * 1024
        ),
        cost_estimate=pl.CostEstimate(flops=flops, bytes_accessed=11 << 20, transcendentals=0),
        name="bddc_apply",
    )(*args)
    return pl.pallas_call(
        functools.partial(store, 4),
        out_shape=(out, out),
        in_specs=[any_, any_],
        out_specs=(any_, any_),
        scratch_shapes=[vmem((n_if, cols), BF16), vmem((n_if, cols), BF16), dma((2, 4)), dma((2, 4))],
        compiler_params=pltpu.CompilerParams(vmem_limit_bytes=60 * 1024 * 1024),
        name="store",
    )(*done)


def solution(mesh):
    placed = (
        P("grp", "sub", None, None),
        P("grp", "sub", None),
        P(),
        P("grp", "sub", None, None),
        P("grp", "sub", None, None),
        P("grp", "sub", None, None),
        P("grp", "sub", None),
        P("grp", None, None),
        P("grp", None, None),
        P("grp", None),
        P(),
    )
    return jax.shard_map(
        functools.partial(shards, mesh.shape["sub"], mesh.shape["grp"]),
        mesh=mesh,
        in_specs=placed,
        out_specs=(P("grp", "sub", None, None), P("grp", "sub", None, None)),
        check_vma=False,
    )
```

```python
import functools

import jax
import jax.numpy as jnp
from jax import lax
from jax.experimental import pallas as pl
from jax.experimental.pallas import tpu as pltpu
from jax.sharding import PartitionSpec as P

MESH = pl.DeviceIdType.MESH
F32 = jnp.float32
BF16 = jnp.bfloat16
LANES = 128


def dot(a, b):
    return jnp.dot(a, b, preferred_element_type=F32)


def dot_t(a, b):
    return lax.dot_general(a, b, (((1,), (1,)), ((), ())), preferred_element_type=F32)


def two_terms(x):
    high = x.astype(BF16)
    low = (x - high.astype(F32)).astype(BF16)
    return jnp.concatenate([high, low], axis=0)


def fold_terms(x):
    half = x.shape[0] // 2
    return x[:half] + x[half:]


def block(index, size):
    return pl.ds(pl.multiple_of(index * size, size), size)


def plane(nsub):
    nx = 4 if nsub % 8 == 0 else 2
    return nx, nsub // (2 * nx)


def far_first(r):
    return r + lax.div(r, 2) - 2 * lax.div(r, 3)


def kernel(
    nsub,
    ngrp,
    resid_h,
    order_h,
    stiff_h,
    schur_h,
    linv_h,
    basis_h,
    cmap_h,
    l2inv_h,
    l2basis_h,
    l2map_h,
    l3inv_h,
    sol_h,
    img_h,
    resid,
    order_s,
    basis_s,
    cmap,
    l2map,
    stiff,
    schur,
    linv,
    l2inv,
    l2basis,
    l3inv,
    l2maps,
    perm_t,
    perm,
    dofw,
    weighted,
    t_src,
    t_recv,
    c_src,
    c_recv,
    recv2,
    onehot2,
    onehot3,
    q3,
    recv3,
    term3,
    back,
    xtwo,
    xcoef,
    xn,
    scaled,
    mine_l,
    theirs_l,
    basis_f,
    basis_n,
    schur_p,
    base,
    pair,
    sol_acc,
    img_acc,
    sol,
    img,
    in_sem,
    out_sem,
    map3_sem,
    t_sem,
    c_sem,
    z_sem,
    back_sem,
    lf_send,
    lf_recv,
    bf_send,
    bf_recv,
    xf_send,
    xf_recv,
    xz_send,
    xz_recv,
):
    grp = lax.axis_index("grp")
    sub = lax.axis_index("sub")
    n_if, cols = weighted.shape
    face = n_if // 4
    nc1 = xcoef.shape[1]
    ng2, nc2 = l2basis.shape
    ng3 = l3inv.shape[0]
    kc = cols // nsub
    half = cols // 2

    loads = [
        pltpu.make_async_copy(src, dst, in_sem.at[i])
        for i, (src, dst) in enumerate(
            [
                (order_h.at[0], order_s),
                (stiff_h, stiff),
                (cmap_h.at[0], cmap),
                (l2map_h, l2map),
                (basis_h.at[0, 0], basis_s),
                (l2basis_h.at[0], l2basis),
                (resid_h.at[0, 0], resid),
                (linv_h.at[0, 0], linv),
                (l2inv_h.at[0], l2inv),
                (l3inv_h, l3inv),
                (schur_h.at[0, 0], schur),
            ]
        )
    ]
    for load in loads[:8]:
        load.start()
    ld_order, ld_stiff, ld_cmap, ld_l2map, ld_basis, ld_l2basis, ld_resid, ld_linv, ld_l2inv, ld_l3inv, ld_schur = loads

    nx, ny = plane(nsub)
    at_y, at_x, at_c = lax.div(sub, 2 * nx), lax.rem(lax.div(sub, 2), nx), lax.rem(sub, 2)

    row = 2 * nx
    far_x = [lax.rem(at_x + d, nx) * 2 for d in ((2, 3, 1, 0) if nx == 4 else (1, 0))]
    far_c = [lax.rem(at_c + d, 2) for d in (1, 0)]

    def row_at(r):
        return lax.rem(at_y + far_first(ny - 1 - r), ny)

    def over_row(y, visit, with_self=False):
        for i, x in enumerate(far_x):
            for j, c in enumerate(far_c):
                t = y * row + x + c
                if with_self or (i, j) != (nx - 1, 1):
                    visit(t)
                else:
                    pl.when(t != sub)(functools.partial(visit, t))

    def over_plane(visit):
        def body(r, carry):
            over_row(row_at(r), visit)
            return carry

        lax.fori_loop(0, ny, body, 0)

    def peer_grp(i):
        off = ngrp // 2 + lax.div(i + 1, 2) * (1 - 2 * lax.rem(i, 2))
        return lax.rem(grp + off, ngrp)

    barrier = pltpu.get_barrier_semaphore()

    def greet_sub(t):
        pl.semaphore_signal(barrier, inc=1, device_id={"sub": t}, device_id_type=MESH)

    def greet_grp(i, carry):
        pl.semaphore_signal(barrier, inc=1, device_id={"grp": peer_grp(i)}, device_id_type=MESH)
        return carry

    over_plane(greet_sub)
    lax.fori_loop(0, ngrp - 1, greet_grp, 0)

    ld_stiff.wait()
    own = stiff[grp, sub]
    exists = [sub > 0, sub < nsub - 1, grp > 0, grp < ngrp - 1]
    weights, their_weights = [], []
    for f, (g, s) in enumerate(((grp, sub - 1), (grp, sub + 1), (grp - 1, sub), (grp + 1, sub))):
        other = stiff[jnp.clip(g, 0, ngrp - 1), jnp.clip(s, 0, nsub - 1)]
        here = jnp.full((8, face), exists[f].astype(jnp.int32), jnp.int32) > 0
        num, nbr = jnp.full((8, face), own, F32), jnp.full((8, face), other, F32)
        weights.append(jnp.where(here, num / (num + nbr), F32(1.0))[0:1])
        their_weights.append((nbr / (nbr + num))[0:1])
    all_weights = jnp.concatenate(weights, axis=1)

    onehot2[:, 0:nc1] = jnp.zeros((ng2, nc1), BF16)
    onehot2[:, (nsub + 1) * nc1 :] = jnp.zeros((ng2, nc1), BF16)
    for f in range(4):

        @pl.when(jnp.logical_not(exists[f]))
        def _(f=f):
            rows = slice(f * face, (f + 1) * face)
            theirs_l[rows, :] = jnp.zeros((face, cols), BF16)
            basis_n[rows, :] = jnp.zeros((face, nc1), BF16)
            xn[f] = jnp.zeros((cols, nc1), BF16)

    ld_cmap.wait()
    ld_l2map.wait()
    l2maps[grp] = jnp.broadcast_to(l2map[...], (8, nc2))
    ld_order.wait()
    order = order_s[...]

    def weigh(r, carry):
        rows = block(r, face)
        ids = lax.broadcasted_iota(jnp.int32, (face, n_if), 0) + r * face
        here = ids == order
        perm_t[rows, :] = jnp.where(here, F32(1.0), F32(0.0)).astype(BF16)
        dw = jnp.sum(jnp.where(here, all_weights, F32(0.0)), axis=1, keepdims=True)
        dofw[rows, :] = jnp.broadcast_to(dw, (face, LANES))
        return carry

    lax.fori_loop(0, 4, weigh, 0)
    ld_basis.wait()
    basis = basis_s[...]
    basis_t = basis.astype(F32).T.astype(BF16)
    ld_l2basis.wait()
    l2basis_t = l2basis[...].T.astype(BF16)
    own_ids = lax.broadcasted_iota(jnp.int32, (ng2, nc1), 0)
    own_map = jnp.where(own_ids == cmap[...], F32(1.0), F32(0.0)).astype(BF16)
    own_rows = dot(l2basis_t, own_map).astype(BF16)
    both_t = jnp.concatenate([basis_t, dot(own_rows, basis_t).astype(BF16)], axis=0)
    ld_resid.wait()
    for load in loads[8:]:
        load.start()
    wide = jnp.concatenate([dofw[...]] * (-(-cols // LANES)), axis=1)[:, :cols]
    weighted[...] = (wide * resid[...].astype(F32)).astype(BF16)
    coarse_t = dot(both_t, weighted[...]).T.astype(BF16)
    t_src[...] = coarse_t[:, nc1:].reshape(nsub, kc, nc2)
    c_src[:, 0:kc, :] = coarse_t[:, :nc1].reshape(nsub, kc, nc1)
    high = lax.shift_right_logical(cmap[...], 8)
    map_rows = jnp.concatenate(
        [high.astype(F32), (cmap[...] - high * 256).astype(F32), jnp.zeros((kc - 2, nc1), F32)], axis=0
    ).astype(BF16)
    c_src[:, kc : 2 * kc, :] = jnp.broadcast_to(map_rows[None], (nsub, kc, nc1))

    pl.semaphore_wait(barrier, nsub + ngrp - 2)

    def wait_bytes(ref, sem):
        pltpu.make_async_copy(ref, ref, sem).wait()

    def send_t(t):
        pltpu.make_async_remote_copy(
            src_ref=t_src.at[t],
            dst_ref=t_recv.at[sub],
            send_sem=t_sem.at[0],
            recv_sem=t_sem.at[1],
            device_id={"sub": t},
            device_id_type=MESH,
        ).start()

    def send_c(t):
        pltpu.make_async_remote_copy(
            src_ref=c_src.at[t],
            dst_ref=c_recv.at[sub],
            send_sem=c_sem.at[0],
            recv_sem=c_sem.at[1],
            device_id={"sub": t},
            device_id_type=MESH,
        ).start()

    def send_map3(i, carry):
        pltpu.make_async_remote_copy(
            src_ref=l2maps.at[grp],
            dst_ref=l2maps.at[grp],
            send_sem=map3_sem.at[0],
            recv_sem=map3_sem.at[1],
            device_id={"grp": peer_grp(i)},
            device_id_type=MESH,
        ).start()
        return carry

    over_plane(send_t)
    lax.fori_loop(0, ngrp - 1, send_map3, 0)
    over_plane(send_c)
    t_recv[sub] = t_src[sub]
    c_recv[sub] = c_src[sub]

    ld_linv.wait()
    scaled[...] = (wide * dot(linv[...], weighted[...])).astype(BF16)
    order_col = jnp.broadcast_to(order.astype(F32), (LANES, n_if)).T.astype(jnp.int32)

    def build_perm(b, carry):
        ids = lax.broadcasted_iota(jnp.int32, (n_if, LANES), 1) + b * LANES
        perm[:, block(b, LANES)] = jnp.where(ids == order_col, F32(1.0), F32(0.0)).astype(BF16)
        return carry

    lax.fori_loop(0, n_if // LANES, build_perm, 0)

    wait_bytes(t_recv.at[pl.ds(0, nsub - 1)], t_sem.at[1])
    term3[...] = jnp.sum(t_recv[...].astype(F32), axis=0)
    recv3[:, block(grp, nc2)] = term3[...]

    def send_z(i, carry):
        pltpu.make_async_remote_copy(
            src_ref=term3,
            dst_ref=recv3.at[:, block(grp, nc2)],
            send_sem=z_sem.at[0],
            recv_sem=z_sem.at[1],
            device_id={"grp": peer_grp(i)},
            device_id_type=MESH,
        ).start()
        return carry

    lax.fori_loop(0, ngrp - 1, send_z, 0)

    mine_l[...] = dot(perm[...], scaled[...]).astype(BF16)
    facing = (1, 0, 3, 2)

    def to_neighbour(f, src, dst, send_sem, recv_sem):
        axis, step = (("sub", -1), ("sub", 1), ("grp", -1), ("grp", 1))[f]
        size = nsub if axis == "sub" else ngrp
        return pltpu.make_async_remote_copy(
            src_ref=src,
            dst_ref=dst,
            send_sem=send_sem,
            recv_sem=recv_sem,
            device_id={axis: jnp.clip(lax.axis_index(axis) + step, 0, size - 1)},
            device_id_type=MESH,
        )

    for f in (2, 3, 0, 1):

        @pl.when(exists[f])
        def _(f=f):
            o = facing[f]
            rows, there = pl.ds(f * face, face), pl.ds(o * face, face)
            to_neighbour(f, mine_l.at[rows], theirs_l.at[there], lf_send.at[f], lf_recv.at[o]).start()

    wait_bytes(l2maps.at[pl.ds(0, ngrp - 1)], map3_sem.at[1])

    def build3(t, carry):
        ids = lax.broadcasted_iota(jnp.int32, (ng3, nc2), 0)
        onehot3[:, block(t, nc2)] = jnp.where(ids == l2maps[t][0:1], F32(1.0), F32(0.0)).astype(BF16)
        return carry

    lax.fori_loop(0, ngrp, build3, 0)
    ld_l3inv.wait()
    own3 = onehot3[:, block(grp, nc2)].astype(F32).T.astype(BF16)
    l3rows = dot(own3, l3inv[...].astype(BF16)).astype(BF16)
    q3[...] = dot(l3rows, onehot3[...]).astype(BF16)

    wait_bytes(c_recv.at[pl.ds(0, nsub - 1)], c_sem.at[1])

    def build2(t, carry):
        recv2[:, block(t, nc1)] = c_recv[t, 0:kc, :]
        parts = c_recv[t, kc : 2 * kc, :].astype(F32)
        ids = lax.broadcasted_iota(jnp.int32, (ng2, nc1), 0)
        member = (parts[0:1] * 256.0 + parts[1:2]).astype(jnp.int32)
        onehot2[:, block(t + 1, nc1)] = jnp.where(ids == member, F32(1.0), F32(0.0)).astype(BF16)
        return carry

    lax.fori_loop(0, nsub, build2, 0)
    ld_l2inv.wait()
    res2 = dot_t(recv2[...], onehot2[:, nc1 : (nsub + 1) * nc1])
    local2 = fold_terms(dot_t(two_terms(res2), l2inv[...].astype(BF16)))

    wait_bytes(recv3.at[:, pl.ds(0, (ngrp - 1) * nc2)], z_sem.at[1])
    picked = two_terms(fold_terms(dot_t(two_terms(recv3[...]), q3[...])))
    sol2 = (local2 + fold_terms(dot(picked, l2basis_t))).astype(BF16)
    odd = lax.rem(sub, 2)

    def two(t):
        return pl.ds(pl.multiple_of((lax.rem(t, row) + lax.rem(t, 2)) * nc1, nc1), 2 * nc1)

    def spread(r, carry):
        y = row_at(r)
        here = pl.ds(pl.multiple_of(y * row * nc1, nc1), (row + 2) * nc1)
        back[y] = dot(sol2, onehot2[:, here]).astype(BF16)

        def send_back(t):
            pltpu.make_async_remote_copy(
                src_ref=back.at[y, :, two(t)],
                dst_ref=xtwo.at[block(sub, kc), :],
                send_sem=back_sem.at[0],
                recv_sem=back_sem.at[1],
                device_id={"sub": t},
                device_id_type=MESH,
            ).start()

        over_row(y, send_back)
        return carry

    lax.fori_loop(0, ny, spread, 0)
    xtwo[block(sub, kc), :] = back[at_y, :, two(sub)]

    def send_across(r, carry):
        y = row_at(r)
        for f, step in ((2, -1), (3, 1)):

            def send(t, f=f, step=step):
                pltpu.make_async_remote_copy(
                    src_ref=back.at[y, :, block(t - y * row + 1, nc1)],
                    dst_ref=xn.at[facing[f], block(sub, kc), :],
                    send_sem=xz_send.at[f - 2],
                    recv_sem=xz_recv.at[facing[f] - 2],
                    device_id={"sub": t, "grp": jnp.clip(grp + step, 0, ngrp - 1)},
                    device_id_type=MESH,
                ).start()

            pl.when(exists[f])(functools.partial(over_row, y, send, True))

        return carry

    lax.fori_loop(0, ny, send_across, 0)

    basis_f[...] = dot(perm[...], basis).astype(BF16)
    for f in (2, 3, 0, 1):

        @pl.when(exists[f])
        def _(f=f):
            o = facing[f]
            rows, there = pl.ds(f * face, face), pl.ds(o * face, face)
            to_neighbour(f, basis_f.at[rows], basis_n.at[there], bf_send.at[f], bf_recv.at[o]).start()

    ld_schur.wait()
    wide_p = n_if // 2
    schur_p[:, 0:wide_p] = dot(schur[...], perm_t[:, 0:wide_p]).astype(BF16)

    wait_bytes(xtwo.at[pl.ds(0, (nsub - 1) * kc), :], back_sem.at[1])
    xcoef[...] = xtwo[:, block(1 - odd, nc1)]
    xn[odd] = xtwo[:, block(odd, nc1)]
    pltpu.make_async_remote_copy(
        src_ref=xcoef,
        dst_ref=xn.at[odd],
        send_sem=xf_send.at[0],
        recv_sem=xf_recv.at[0],
        device_id={"sub": sub + 1 - 2 * odd},
        device_id_type=MESH,
    ).start()

    schur_p[:, wide_p:] = dot(schur[...], perm_t[:, wide_p:]).astype(BF16)

    for f in range(4):

        @pl.when(exists[f])
        def _(f=f):
            wait_bytes(theirs_l.at[pl.ds(f * face, face)], lf_recv.at[f])
            wait_bytes(basis_n.at[pl.ds(f * face, face)], bf_recv.at[f])

        rows = slice(f * face, (f + 1) * face)
        base[rows, :] = mine_l[rows, :].astype(F32) + theirs_l[rows, :].astype(F32)
        pair[rows, 0:nc1] = (weights[f][:, 0:1] * basis_f[rows, :].astype(F32)).astype(BF16)
        pair[rows, nc1:] = (their_weights[f][:, 0:1] * basis_n[rows, :].astype(F32)).astype(BF16)

    def summed(f, here):
        rows = slice(f * face, (f + 1) * face)
        both = jnp.concatenate([xcoef[here, :], xn[f, here, :]], axis=1)
        return (base[rows, here] + dot_t(pair[rows, :], both)).astype(BF16)

    wait_bytes(xn.at[1 - odd], xf_recv.at[0])
    lower = jnp.concatenate([summed(0, slice(0, cols)), summed(1, slice(0, cols))], axis=0)
    sol_acc[...] = dot(perm_t[:, 0 : 2 * face], lower).astype(BF16)
    img_acc[...] = dot(schur_p[:, 0 : 2 * face], lower)

    for f in (2, 3):

        @pl.when(exists[f])
        def _(f=f):
            wait_bytes(xn.at[f], xz_recv.at[f - 2])

    stores = []
    for h in range(2):
        here = slice(h * half, (h + 1) * half)
        upper = jnp.concatenate([summed(2, here), summed(3, here)], axis=0)
        there = pl.ds(h * half, half)
        sol[:, here] = (sol_acc[:, here].astype(F32) + dot(perm_t[:, 2 * face :], upper)).astype(BF16)
        stores.append(pltpu.make_async_copy(sol.at[:, there], sol_h.at[0, 0, :, there], out_sem.at[0, h]))
        stores[-1].start()
        img[:, here] = (img_acc[:, here] + dot(schur_p[:, 2 * face :], upper)).astype(BF16)
        stores.append(pltpu.make_async_copy(img.at[:, there], img_h.at[0, 0, :, there], out_sem.at[1, h]))
        stores[-1].start()

    wait_bytes(t_src.at[pl.ds(0, nsub - 1)], t_sem.at[0])
    wait_bytes(c_src.at[pl.ds(0, nsub - 1)], c_sem.at[0])
    wait_bytes(l2maps.at[pl.ds(0, ngrp - 1)], map3_sem.at[0])
    wait_bytes(recv3.at[:, pl.ds(0, (ngrp - 1) * nc2)], z_sem.at[0])
    wait_bytes(xtwo.at[pl.ds(0, (nsub - 1) * kc), :], back_sem.at[0])
    wait_bytes(xcoef, xf_send.at[0])
    for f in range(4):

        @pl.when(exists[f])
        def _(f=f):
            rows = pl.ds(f * face, face)
            wait_bytes(mine_l.at[rows], lf_send.at[f])
            wait_bytes(basis_f.at[rows], bf_send.at[f])
            if f >= 2:
                wait_bytes(xn.at[f], xz_send.at[f - 2])

    for done in stores:
        done.wait()


def store(parts, sol, img, sol_h, img_h, sol_v, img_v, in_sem, out_sem):
    size = sol_v.shape[0] // parts
    moves = []
    for i in range(parts):
        rows = pl.ds(i * size, size)
        for j, (src, via, dst) in enumerate([(sol, sol_v, sol_h), (img, img_v, img_h)]):
            load = pltpu.make_async_copy(src.at[0, 0, rows], via.at[rows], in_sem.at[j, i])
            moves.append((load, pltpu.make_async_copy(via.at[rows], dst.at[0, 0, rows], out_sem.at[j, i])))
            load.start()
    for load, save in moves:
        load.wait()
        save.start()
    for load, save in moves:
        save.wait()


def shards(nsub, ngrp, *args):
    resid, order, stiff, schur, linv, basis, cmap, l2inv, l2basis, l2map, l3inv = args
    n_if, cols = resid.shape[2:]
    nc1 = basis.shape[3]
    ng2, nc2 = l2basis.shape[1:]
    ng3 = l3inv.shape[0]
    kc = cols // nsub
    nx, ny = plane(nsub)
    vmem = pltpu.VMEM
    dma = pltpu.SemaphoreType.DMA
    scratch = [
        vmem((n_if, cols), BF16),
        vmem((1, n_if), jnp.int32),
        vmem((n_if, nc1), BF16),
        vmem((1, nc1), jnp.int32),
        vmem((1, nc2), jnp.int32),
        pltpu.SMEM((ngrp, nsub), F32),
        vmem((n_if, n_if), BF16),
        vmem((n_if, n_if), BF16),
        vmem((ng2, ng2), F32),
        vmem((ng2, nc2), F32),
        vmem((ng3, ng3), F32),
        vmem((ngrp, 8, nc2), jnp.int32),
        vmem((n_if, n_if), BF16),
        vmem((n_if, n_if), BF16),
        vmem((n_if, LANES), F32),
        vmem((n_if, cols), BF16),
        vmem((nsub, kc, nc2), BF16),
        vmem((nsub, kc, nc2), BF16),
        vmem((nsub, 2 * kc, nc1), BF16),
        vmem((nsub, 2 * kc, nc1), BF16),
        vmem((kc, nsub * nc1), BF16),
        vmem((ng2, (nsub + 2) * nc1), BF16),
        vmem((ng3, ngrp * nc2), BF16),
        vmem((nc2, ngrp * nc2), BF16),
        vmem((kc, ngrp * nc2), F32),
        vmem((kc, nc2), F32),
        vmem((ny, kc, (2 * nx + 2) * nc1), BF16),
        vmem((cols, 2 * nc1), BF16),
        vmem((cols, nc1), BF16),
        vmem((4, cols, nc1), BF16),
        vmem((n_if, cols), BF16),
        vmem((n_if, cols), BF16),
        vmem((n_if, cols), BF16),
        vmem((n_if, nc1), BF16),
        vmem((n_if, nc1), BF16),
        vmem((n_if, n_if), BF16),
        vmem((n_if, cols), F32),
        vmem((n_if, 2 * nc1), BF16),
        vmem((n_if, cols), BF16),
        vmem((n_if, cols), F32),
        vmem((n_if, cols), BF16),
        vmem((n_if, cols), BF16),
        dma((11,)),
        dma((2, 2)),
        dma((2,)),
        dma((2,)),
        dma((2,)),
        dma((2,)),
        dma((2,)),
        dma((4,)),
        dma((4,)),
        dma((4,)),
        dma((4,)),
        dma((1,)),
        dma((1,)),
        dma((2,)),
        dma((2,)),
    ]
    flops = 2 * n_if * cols * n_if * 4 + 2 * n_if**3
    out = jax.ShapeDtypeStruct((1, 1, n_if, cols), BF16)
    any_ = pl.BlockSpec(memory_space=pl.ANY)
    done = pl.pallas_call(
        functools.partial(kernel, nsub, ngrp),
        out_shape=(out, out),
        in_specs=[any_] * 11,
        out_specs=(any_, any_),
        scratch_shapes=scratch,
        compiler_params=pltpu.CompilerParams(
            collective_id=0, has_side_effects=True, vmem_limit_bytes=60 * 1024 * 1024
        ),
        cost_estimate=pl.CostEstimate(flops=flops, bytes_accessed=11 << 20, transcendentals=0),
        name="bddc_apply",
    )(*args)
    return pl.pallas_call(
        functools.partial(store, 4),
        out_shape=(out, out),
        in_specs=[any_, any_],
        out_specs=(any_, any_),
        scratch_shapes=[vmem((n_if, cols), BF16), vmem((n_if, cols), BF16), dma((2, 4)), dma((2, 4))],
        compiler_params=pltpu.CompilerParams(vmem_limit_bytes=60 * 1024 * 1024),
        name="store",
    )(*done)


def solution(mesh):
    placed = (
        P("grp", "sub", None, None),
        P("grp", "sub", None),
        P(),
        P("grp", "sub", None, None),
        P("grp", "sub", None, None),
        P("grp", "sub", None, None),
        P("grp", "sub", None),
        P("grp", None, None),
        P("grp", None, None),
        P("grp", None),
        P(),
    )
    return jax.shard_map(
        functools.partial(shards, mesh.shape["sub"], mesh.shape["grp"]),
        mesh=mesh,
        in_specs=placed,
        out_specs=(P("grp", "sub", None, None), P("grp", "sub", None, None)),
        check_vma=False,
    )
```
